128 devices in a mesh: dp: 8 (over z, core), seq: 16 (over y, x).
Axes of the slice: x: 4, y: 4, z: 4, core: 2. Of those that a mesh axis runs over, the one named last changes fastest.
Arguments:
- query_pre: bfloat16 [16, 1024, 6144], P('dp', 'seq'), may hold values from -16 to 16
- key_pre: bfloat16 [16, 1024, 6144], P('dp', 'seq'), may hold values from -16 to 16
- saved_values: bfloat16 [16, 1024, 6144], P('dp', 'seq'), may hold values from -6 to 6
- out_grad: bfloat16 [16, 1024, 6144], P('dp', 'seq'), may hold values from -6 to 6
- out_weight: bfloat16 [6144, 6144], P('seq'), may hold values from -0.078125 to 0.078125
- visible: int32 [16, 1024], P('dp', 'seq'), may hold values from 0 to 4095, as said below
Outputs:
- query_grad: bfloat16 [16, 1024, 6144], P('dp', 'seq')
- key_grad: bfloat16 [16, 1024, 6144], P('dp', 'seq')
- value_grad: bfloat16 [16, 1024, 6144], P('dp', 'seq')
- weight_grad: float32 [6144, 6144], P(('seq', 'dp'))
The draws below stay inside these ranges and needn't reach their ends.
Inputs may be any that keep to these rules, and one draw needn't show every extreme that they name: `visible`: the 1024 patch numbers of a sample are distinct; 0 and 4095 are among them in every sample.
All inputs are finite; a program needn't handle non-finite values.
Results may differ from the reference program's by a relative error of at most 0.017.
The reference program's roundings to bfloat16 on the way count: a program that leaves them out, or rounds other values in their place, can miss the bound.
Values may be sent and summed in bfloat16 or wider, within the bound.
A program may use at most 192 MiB of HBM per device.

```python
import math
import jax
import jax.numpy as jnp
from jax import lax

HEADS = 48
HEAD = 128
D = 6144
GRID = 64
PATCHES = 4096
VIS = 1024
SAMPLES = 16


def draw_query_pre(key, part):
    key = jax.random.fold_in(key, 11)
    full_shape = (SAMPLES, VIS, HEADS * HEAD)
    return jnp.clip(jax.random.normal(key, full_shape, jnp.float32), -6.0, 6.0).astype(jnp.bfloat16)


def draw_key_pre(key, part):
    key = jax.random.fold_in(key, 23)
    full_shape = (SAMPLES, VIS, HEADS * HEAD)
    return jnp.clip(jax.random.normal(key, full_shape, jnp.float32), -6.0, 6.0).astype(jnp.bfloat16)


def draw_visible(key, part):
    key = jax.random.fold_in(key, 37)
    sample_keys = jax.random.split(key, SAMPLES)

    def one_sample(sample_key):
        first_key, second_key = jax.random.split(sample_key)
        middle = jax.random.permutation(first_key, PATCHES - 2)[:VIS - 2].astype(jnp.int32) + 1
        chosen = jnp.concatenate([jnp.array([0, PATCHES - 1], dtype=jnp.int32), middle])
        return jax.random.permutation(second_key, chosen)
    return jax.vmap(one_sample)(sample_keys)


def steps_of(stream_key, dims, pieces, least, high):
    def one(position, blocks):
        steps = jax.random.uniform(jax.random.fold_in(jax.random.fold_in(stream_key, 6), position), (blocks,), jnp.float32, least / len(pieces), high / len(pieces))
        return jnp.repeat(jnp.exp(steps), dims[position] // blocks).reshape((-1,) + (1,) * (len(dims) - position - 1))

    factor_of = one(*pieces[0])
    for cut in pieces[1:]:
        factor_of = factor_of * one(*cut)
    return factor_of


def noise(stream_key, dims, scale, most, cuts=(), kind=jnp.bfloat16):
    drawn = scale * jax.random.normal(stream_key, dims, jnp.float32)
    if cuts:
        drawn = drawn * steps_of(stream_key, dims, cuts, -0.22, 0.18)
    return jnp.clip(drawn, -most, most).astype(kind)


def setup_inputs(seed: int = 0) -> dict:
    streams_of = jax.random.split(jax.random.key(seed), 7)
    return {
        "query_pre": draw_query_pre(jax.random.fold_in(streams_of[6], 71), 0),
        "key_pre": draw_key_pre(jax.random.fold_in(streams_of[6], 71), 0),
        "saved_values": noise(streams_of[2], (SAMPLES, VIS, D), 1.0, 6.0, ((0, 8), (1, 16))),
        "out_grad": noise(streams_of[3], (SAMPLES, VIS, D), 1.0, 6.0, ((0, 8), (1, 16))),
        "out_weight": noise(streams_of[4], (D, D), D ** -0.5, 0.078125, ((0, 16),)),
        "visible": draw_visible(jax.random.fold_in(streams_of[6], 71), 0),
    }


def position_angles(visible, head_size):
    quarter = head_size // 8
    row_index = (visible // GRID).astype(jnp.float32)
    col_index = (visible % GRID).astype(jnp.float32)
    frequency = jnp.exp(jnp.arange(quarter, dtype=jnp.float32) * (-math.log(100.0) / quarter))
    return (row_index[..., None] * frequency, col_index[..., None] * frequency)

def rotate(tensor, visible, direction):
    head_size = tensor.shape[-1]
    quarter = head_size // 8
    row_angle, col_angle = position_angles(visible, head_size)

    def turn(first_half, second_half, angles):
        cosine = jnp.cos(angles)[:, :, None, :]
        sine_part = direction * jnp.sin(angles)[:, :, None, :]
        return (first_half * cosine - second_half * sine_part, first_half * sine_part + second_half * cosine)
    row_first, row_second = turn(tensor[..., :quarter], tensor[..., quarter:2 * quarter], row_angle)
    col_first, col_second = turn(tensor[..., 2 * quarter:3 * quarter], tensor[..., 3 * quarter:4 * quarter], col_angle)
    return jnp.concatenate([row_first, row_second, col_first, col_second, tensor[..., 4 * quarter:]], axis=-1)

def rotate_tokens(tokens_in, visible, direction):
    seq_count, token_count, model_width = tokens_in.shape
    split = tokens_in.astype(jnp.float32).reshape(seq_count, token_count, model_width // HEAD, HEAD)
    return rotate(split, visible, direction).astype(jnp.bfloat16).reshape(seq_count, token_count, model_width)

def attend_forward(query_rows, rotated_key_rows, value_rows):
    score_scale = 1.0 / math.sqrt(query_rows.shape[-1])
    scores = jnp.dot(query_rows, rotated_key_rows.T, preferred_element_type=jnp.float32) * score_scale
    row_max = lax.optimization_barrier(jnp.max(scores, axis=-1, keepdims=True))
    expon = jnp.exp(scores - row_max)
    attention_weights = expon / lax.optimization_barrier(jnp.sum(expon, axis=-1, keepdims=True))
    attended = jnp.dot(attention_weights.astype(jnp.bfloat16), value_rows, preferred_element_type=jnp.float32).astype(jnp.bfloat16)
    return (attention_weights, attended)

def attend_backward(query_rows, rotated_key_rows, value_rows, attention_weights, attended, output_gradient_rows):
    score_scale = 1.0 / math.sqrt(query_rows.shape[-1])
    reduced_precision_weights = attention_weights.astype(jnp.bfloat16)
    value_part = jnp.dot(reduced_precision_weights.T, output_gradient_rows, preferred_element_type=jnp.float32).astype(jnp.bfloat16)
    probability_gradient = jnp.dot(output_gradient_rows, value_rows.T, preferred_element_type=jnp.float32)
    row_dot = lax.optimization_barrier(jnp.sum(output_gradient_rows.astype(jnp.float32) * attended.astype(jnp.float32), axis=-1, keepdims=True))
    score_gradient = (attention_weights * (probability_gradient - row_dot)).astype(jnp.bfloat16)
    query_part = (jnp.dot(score_gradient, rotated_key_rows, preferred_element_type=jnp.float32) * score_scale).astype(jnp.bfloat16)
    key_part = (jnp.dot(score_gradient.T, query_rows, preferred_element_type=jnp.float32) * score_scale).astype(jnp.bfloat16)
    return (query_part, key_part, value_part)

def reference(query_pre, key_pre, saved_values, out_grad, out_weight, visible):
    samples, seq_length, model_width = query_pre.shape
    head_count = model_width // HEAD
    query_rows = rotate_tokens(query_pre, visible, 1.0)
    rotated_key_rows = rotate_tokens(key_pre, visible, 1.0)
    output_gradient_rows = jnp.dot(out_grad.reshape(-1, model_width), out_weight.T, preferred_element_type=jnp.float32)
    output_gradient_rows = output_gradient_rows.astype(jnp.bfloat16).reshape(samples, seq_length, model_width)

    def to_items(tensor):
        return tensor.reshape(samples, seq_length, head_count, HEAD).transpose(0, 2, 1, 3).reshape(samples * head_count, seq_length, HEAD)

    def from_items(tensor):
        return tensor.reshape(samples, head_count, seq_length, HEAD).transpose(0, 2, 1, 3).reshape(samples, seq_length, model_width)

    def per_item(operands):
        query_item, key_item, value_item, dir_item = operands
        attention_weights, attended = attend_forward(query_item, key_item, value_item)
        query_part, key_part, value_part = attend_backward(query_item, key_item, value_item, attention_weights, attended, dir_item)
        return (attended, query_part, key_part, value_part)
    attended, query_part, key_part, value_part = lax.map(per_item, (to_items(query_rows), to_items(rotated_key_rows), to_items(saved_values), to_items(output_gradient_rows)))
    attended_all = from_items(attended)
    weight_grad = jnp.dot(attended_all.reshape(-1, model_width).T, out_grad.reshape(-1, model_width), preferred_element_type=jnp.float32)
    query_grad = rotate_tokens(from_items(query_part), visible, -1.0)
    key_grad = rotate_tokens(from_items(key_part), visible, -1.0)
    return (query_grad, key_grad, from_items(value_part), weight_grad)
```

```python
import functools
import math

import jax
import jax.numpy as jnp
from jax import lax
from jax.experimental import pallas as pl
from jax.experimental.pallas import tpu as pltpu
from jax.sharding import PartitionSpec as P

HEAD = 128
GRID = 64
SIDE = 4
GROUP = SIDE * SIDE
MESH = pl.DeviceIdType.MESH
F32 = jnp.float32
BF16 = jnp.bfloat16
MIB = 1024 * 1024
NT = (((1,), (1,)), ((), ()))
TN = (((0,), (0,)), ((), ()))


def dot(a, b, dims=(((1,), (0,)), ((), ()))):
    return lax.dot_general(a, b, dims, preferred_element_type=F32)


def turn(x, cosine, sine):
    lane = lax.broadcasted_iota(jnp.int32, x.shape, 1)
    quarter = HEAD // 8
    ahead = pltpu.roll(x, HEAD - quarter, 1)
    behind = pltpu.roll(x, quarter, 1)
    partner = jnp.where((lane // quarter) % 2 == 0, ahead, behind)
    return x * cosine + partner * sine


def remote(src, dst, send, recv, target):
    return pltpu.make_async_remote_copy(
        src_ref=src,
        dst_ref=dst,
        send_sem=send,
        recv_sem=recv,
        device_id={"seq": target},
        device_id_type=MESH,
    )


def enter(me):
    barrier = pltpu.get_barrier_semaphore()

    def greet(off, carry):
        pl.semaphore_signal(
            barrier, inc=1, device_id={"seq": lax.rem(me + off, GROUP)}, device_id_type=MESH
        )
        return carry

    lax.fori_loop(1, GROUP, greet, 0)
    pl.semaphore_wait(barrier, GROUP - 1)


def rows_of(block, size):
    return pl.ds(pl.multiple_of(block * size, size), size)


def gather_kernel(
    q_in, k_in, v_in, g_in, w_in, vis_in, pos_in,
    q_out, k_out, v_out, do_out, att_out, lse_out, cos_out, sin_out, wg_out,
    qb, kb, vb, gb, wb, visb, cosb, sinb, att, dot_t, lse, acc, stage,
    a2a_send, a2a_recv, ag_send, ag_recv, local_sem, out_sem,
):
    me = lax.axis_index("seq")
    px, py = lax.rem(me, SIDE), lax.div(me, SIDE)
    samples, local = q_in.shape[0], q_in.shape[1]
    width = q_in.shape[2] // GROUP
    heads = width // HEAD
    tokens = local * GROUP
    part = tokens // SIDE
    model = g_in.shape[2]
    scale = math.log2(math.e) / math.sqrt(HEAD)

    def at(axis, delta, axis2=None, delta2=0):
        x, y = px, py
        for a, d in ((axis, delta), (axis2, delta2)):
            if a == 0:
                x = lax.rem(x + d, SIDE)
            elif a == 1:
                y = lax.rem(y + d, SIDE)
        return y * SIDE + x

    local_copies = [
        pltpu.make_async_copy(w_in, wb, local_sem.at[0]),
        pltpu.make_async_copy(g_in, gb.at[:, rows_of(me, local), :], local_sem.at[1]),
        pltpu.make_async_copy(vis_in, visb.at[me], local_sem.at[2]),
    ]
    for t, (src, dst) in enumerate(((q_in, qb), (k_in, kb), (v_in, vb))):
        local_copies.append(
            pltpu.make_async_copy(
                src.at[:, :, rows_of(me, width)], dst.at[:, rows_of(me, local), :], local_sem.at[3 + t]
            )
        )
    for copy in local_copies:
        copy.start()

    enter(me)

    dirs = (1, SIDE - 1)
    mid = local // 2

    def half_rows(block, which):
        return pl.ds(pl.multiple_of(block * local + which * mid, mid), mid)

    def ag_copy(half, slot, direction, stage_index, block, axis, from_input=False):
        if stage_index == 0:
            place = rows_of(block, local)
        else:
            place = half_rows(block, direction)
        dst = gb.at[half, place, :]
        src = g_in.at[half] if from_input else dst
        return remote(
            src, dst,
            ag_send.at[half, slot, direction, stage_index],
            ag_recv.at[half, slot, direction, stage_index],
            at(axis, dirs[direction]),
        )

    started = []

    def begin(*args, **kwargs):
        copy = ag_copy(*args, **kwargs)
        copy.start()
        started.append(copy)

    def first_direct(half, direction):
        begin(half, 0, direction, 0, me, half, from_input=True)

    def second_direct(half, b):
        for direction in range(2):
            begin(half, 1 + b, direction, 0, at(half, b), 1 - half, from_input=b == 0)

    def got_first(half, direction):
        block = at(half, SIDE - dirs[direction])
        ag_copy(half, 0, direction, 0, block, half).wait_recv()
        begin(half, 0, direction, 1, block, half)
        second_direct(half, (SIDE - dirs[direction]) % SIDE)

    def got_first_far(half):
        block = at(half, 2)
        for direction in range(2):
            ag_copy(half, 0, direction, 1, block, half).wait_recv()
        second_direct(half, 2)

    def got_second(half, b):
        for direction in range(2):
            block = at(half, b, 1 - half, SIDE - dirs[direction])
            ag_copy(half, 1 + b, direction, 0, block, 1 - half).wait_recv()
            begin(half, 1 + b, direction, 1, block, 1 - half)

    def got_second_far(half, b):
        block = at(half, b, 1 - half, 2)
        for direction in range(2):
            ag_copy(half, 1 + b, direction, 1, block, 1 - half).wait_recv()

    for half in range(2):
        for direction in range(2):
            first_direct(half, direction)
    for half in range(2):
        second_direct(half, 0)

    pairs = ((q_in, qb), (k_in, kb), (v_in, vb))

    def send_vis(off, carry):
        target = lax.rem(me + off, GROUP)
        remote(vis_in, visb.at[me], a2a_send.at[3], a2a_recv.at[3], target).start()
        return carry

    lax.fori_loop(1, GROUP, send_vis, 0)
    for t, (src, dst) in enumerate(pairs):

        def send_one(off, carry, src=src, dst=dst, t=t):
            target = lax.rem(me + off, GROUP)
            remote(
                src.at[:, :, rows_of(target, width)],
                dst.at[:, rows_of(me, local), :],
                a2a_send.at[t], a2a_recv.at[t], target,
            ).start()
            return carry

        lax.fori_loop(1, GROUP, send_one, 0)

    def a2a_wait(t, sem, ref):
        view = ref.at[:, pl.ds(0, tokens - local), :] if t < 3 else ref.at[pl.ds(0, GROUP - 1)]
        pltpu.make_async_copy(view, view, sem.at[t]).wait()

    for copy in local_copies:
        copy.wait()

    for half in range(2):
        for direction in range(2):
            got_first(half, direction)
    for half in range(2):
        got_second(half, 0)

    a2a_wait(3, a2a_recv, visb)

    def tables(src, carry):
        seen = visb[src, 0:1, :]
        row, col = lax.div(seen, GRID), lax.rem(seen, GRID)
        place = lax.broadcasted_iota(jnp.int32, (HEAD, 2 * local), 0)
        hot = jnp.where((place == row) | (place == col + GRID), 1.0, 0.0)
        both = lax.dot_general(
            hot, pos_in[...], TN, preferred_element_type=F32, precision=lax.Precision.HIGHEST
        )
        for s in range(samples):
            rows = both[s * local:(s + 1) * local]
            cosb[s, rows_of(src, local), :] = rows[:, :HEAD]
            sinb[s, rows_of(src, local), :] = rows[:, HEAD:]
        return carry

    lax.fori_loop(0, GROUP, tables, 0)
    for t, (_, dst) in enumerate(pairs):
        a2a_wait(t, a2a_recv, dst)

    chunk = 256

    def forward(s, h):
        lanes = slice(h * HEAD, (h + 1) * HEAD)
        cosine, sine = cosb[s], sinb[s]
        qb[s, :, lanes] = turn(qb[s, :, lanes].astype(F32), cosine, sine).astype(BF16)
        kb[s, :, lanes] = turn(kb[s, :, lanes].astype(F32), cosine, sine).astype(BF16)
        values_t = vb[s, :, lanes].astype(F32).T.astype(BF16)

        def one(c, carry):
            place = rows_of(c, chunk)
            scores = dot(kb[s, :, lanes], qb[s, place, lanes], NT) * scale
            top = jnp.max(scores, axis=0, keepdims=True)
            expon = jnp.exp2(scores - top)
            total = jnp.sum(expon, axis=0, keepdims=True)
            probs = (expon * (1.0 / total)).astype(BF16)
            att[s, lanes, place] = dot(values_t, probs).astype(BF16)
            lse[s * heads + h:s * heads + h + 1, place] = top + jnp.log2(total)
            return carry

        lax.fori_loop(0, tokens // chunk, one, 0)

    def out_dir(s, row):
        place = rows_of(row, part)
        dot_t[s, :, place] = dot(wb[...], gb[s, place, :], NT).astype(BF16)

    tile = stage.shape[2]

    def weight_part(row, first=False, last=False):
        place = rows_of(row, part)

        def put(j, slot):
            return pltpu.make_async_copy(
                stage.at[slot], wg_out.at[:, rows_of(j, tile)], out_sem.at[slot]
            )

        def one(j, carry):
            cols = rows_of(j, tile)
            total = dot(att[0, :, place], gb[0, place, cols])
            for s in range(1, samples):
                total += dot(att[s, :, place], gb[s, place, cols])
            if not first:
                total += acc[:, cols]
            if last:
                slot = lax.rem(j, 2)

                @pl.when(j >= 2)
                def _():
                    put(j - 2, slot).wait()

                stage[slot] = total.astype(BF16)
                put(j, slot).start()
            else:
                acc[:, cols] = total
            return carry

        steps = model // tile
        lax.fori_loop(0, steps, one, 0)
        if last:
            for j in (steps - 2, steps - 1):
                put(j, j % 2).wait()

    near = [lax.rem(py + d, SIDE) for d in range(SIDE)]

    forward(0, 0)
    for half in range(2):
        got_first_far(half)
    forward(0, 1)
    for b in (1, SIDE - 1):
        for half in range(2):
            got_second(half, b)
        forward(*((0, 2) if b == 1 else (1, 0)))
    for half in range(2):
        got_second_far(half, 0)
    out_dir(0, near[0])
    out_dir(1, near[0])
    for half in range(2):
        got_second(half, 2)
    forward(1, 1)
    forward(1, 2)
    weight_part(near[0], first=True)
    for b in (1, SIDE - 1):
        for half in range(2):
            got_second_far(half, b)
        out_dir(0, near[b])
        out_dir(1, near[b])
        weight_part(near[b])
    outs = [
        pltpu.make_async_copy(src, dst, out_sem.at[2 + i])
        for i, (src, dst) in enumerate(
            (
                (qb, q_out), (kb, k_out), (vb, v_out), (att, att_out),
                (lse, lse_out), (cosb, cos_out), (sinb, sin_out),
            )
        )
    ]
    for copy in outs:
        copy.start()
    for half in range(2):
        got_second_far(half, 2)
    out_dir(0, near[2])
    out_dir(1, near[2])
    last = pltpu.make_async_copy(dot_t, do_out, out_sem.at[2 + len(outs)])
    last.start()
    weight_part(near[2], last=True)
    last.wait()
    for copy in outs:
        copy.wait()
    for copy in started:
        copy.wait_send()
    for t, (_, dst) in enumerate(pairs):
        a2a_wait(t, a2a_send, dst)
    a2a_wait(3, a2a_send, visb)


def backward_kernel(
    q_in, k_in, v_in, do_in, att_in, lse_in, cos_in, sin_in,
    dq_out, dk_out, dv_out,
    qb, kb, vb, dob, attb, lseb, cosb, sinb, dqb, dkb, dvb, dka, dva, kt,
    load_sem, send_sem, recv_sem, own_sem,
):
    me = lax.axis_index("seq")
    samples, tokens, width = q_in.shape
    heads = width // HEAD
    local = tokens // GROUP
    scale = 1.0 / math.sqrt(HEAD)
    scale2 = math.log2(math.e) / math.sqrt(HEAD)
    chunk = 256

    def loads(s):
        return [
            pltpu.make_async_copy(src.at[s], dst.at[s], load_sem.at[s, i])
            for i, (src, dst) in enumerate(
                (
                    (q_in, qb), (k_in, kb), (v_in, vb), (do_in, dob),
                    (att_in, attb), (cos_in, cosb), (sin_in, sinb),
                )
            )
        ]

    shared = pltpu.make_async_copy(lse_in, lseb, load_sem.at[samples, 0])
    shared.start()
    for s in range(samples):
        for copy in loads(s):
            copy.start()
    enter(me)
    shared.wait()

    outs = ((dqb, dq_out), (dkb, dk_out), (dvb, dv_out))

    def item(s, h):
        lanes = slice(h * HEAD, (h + 1) * HEAD)
        row = s * heads + h
        kt[...] = kb[s, :, lanes].astype(F32).T.astype(BF16)
        dka[...] = jnp.zeros_like(dka)
        dva[...] = jnp.zeros_like(dva)

        def one(c, carry):
            place = rows_of(c, chunk)
            queries = qb[s, place, lanes]
            scores = dot(kb[s, :, lanes], queries, NT)
            probs = jnp.exp2(scores * scale2 - lseb[row:row + 1, place])
            into_t = dob[s, lanes, place]
            into_f = into_t.astype(F32)
            into = into_f.T.astype(BF16)
            row_dot = jnp.sum(into_f * attb[s, lanes, place].astype(F32), axis=0, keepdims=True)
            dprobs = dot(vb[s, :, lanes], into_t)
            dscores = (probs * (dprobs - row_dot)).astype(BF16)
            dva[...] += dot(probs.astype(BF16), into)
            dka[...] += dot(dscores, queries)
            dq = (dot(kt[...], dscores).T * scale).astype(BF16).astype(F32)
            dqb[s, place, lanes] = turn(dq, cosb[s, place, :], -sinb[s, place, :]).astype(BF16)
            return carry

        lax.fori_loop(0, tokens // chunk, one, 0)
        dvb[s, :, lanes] = dva[...].astype(BF16)
        dk = (dka[...] * scale).astype(BF16).astype(F32)
        dkb[s, :, lanes] = turn(dk, cosb[s], -sinb[s]).astype(BF16)

    def ship(s, h, count):
        lanes = slice(h * HEAD, (h + count) * HEAD)
        cols = pl.ds(pl.multiple_of(me * width + h * HEAD, HEAD), count * HEAD)
        for t, (src, dst) in enumerate(outs):

            def send_one(off, carry, src=src, dst=dst, t=t):
                target = lax.rem(me + off, GROUP)
                remote(
                    src.at[s, rows_of(target, local), lanes], dst.at[s, :, cols],
                    send_sem.at[t], recv_sem.at[t], target,
                ).start()
                return carry

            lax.fori_loop(1, GROUP, send_one, 0)
            pltpu.make_async_copy(
                src.at[s, rows_of(me, local), lanes], dst.at[s, :, cols], own_sem.at[t]
            ).start()

    for s in range(samples):
        for copy in loads(s):
            copy.wait()
        for h in range(heads):
            item(s, h)
            ship(s, h, 1)

    for t, (src, dst) in enumerate(outs):
        own = dst.at[:, :, pl.ds(0, width)]
        pltpu.make_async_copy(own, own, own_sem.at[t]).wait()
        rest = dst.at[:, :, pl.ds(width, (GROUP - 1) * width)]
        pltpu.make_async_copy(rest, rest, recv_sem.at[t]).wait()
        pltpu.make_async_copy(rest, rest, send_sem.at[t]).wait()


def position_table():
    quarter = HEAD // 8
    frequency = jnp.exp(jnp.arange(quarter, dtype=F32) * (-math.log(100.0) / quarter))
    angle = jnp.arange(GRID, dtype=F32)[:, None] * frequency
    cosine, sine = jnp.cos(angle), jnp.sin(angle)
    none = jnp.zeros((GRID, 2 * quarter), F32)
    rest = jnp.zeros((GRID, HEAD - 4 * quarter), F32)
    row_cos = jnp.concatenate([cosine, cosine, none, rest + 1.0], axis=1)
    col_cos = jnp.concatenate([none, cosine, cosine, rest], axis=1)
    row_sin = jnp.concatenate([-sine, sine, none, rest], axis=1)
    col_sin = jnp.concatenate([none, -sine, sine, rest], axis=1)
    return jnp.concatenate(
        [
            jnp.concatenate([row_cos, row_sin], axis=1),
            jnp.concatenate([col_cos, col_sin], axis=1),
        ],
        axis=0,
    )


def body(query_pre, key_pre, saved_values, out_grad, out_weight, visible):
    samples, local, model = query_pre.shape
    width = model // GROUP
    tokens = local * GROUP
    hbm = pl.BlockSpec(memory_space=pl.ANY)
    vmem = pl.BlockSpec(memory_space=pltpu.VMEM)
    seen = jnp.broadcast_to(visible.reshape(1, samples * local), (8, samples * local))
    item_shape = (samples, tokens, width)
    turned_shape = (samples, width, tokens)
    table_shape = (samples, tokens, HEAD)
    table = position_table()
    dma = pltpu.SemaphoreType.DMA
    q, k, v, do_t, att_t, lse, cosine, sine, partial = pl.pallas_call(
        gather_kernel,
        out_shape=[
            jax.ShapeDtypeStruct(item_shape, BF16),
            jax.ShapeDtypeStruct(item_shape, BF16),
            jax.ShapeDtypeStruct(item_shape, BF16),
            jax.ShapeDtypeStruct(turned_shape, BF16),
            jax.ShapeDtypeStruct(turned_shape, BF16),
            jax.ShapeDtypeStruct((8, tokens), F32),
            jax.ShapeDtypeStruct(table_shape, F32),
            jax.ShapeDtypeStruct(table_shape, F32),
            jax.ShapeDtypeStruct((width, model), BF16),
        ],
        in_specs=[hbm] * 6 + [vmem],
        out_specs=[hbm] * 9,
        scratch_shapes=[
            pltpu.VMEM(item_shape, BF16),
            pltpu.VMEM(item_shape, BF16),
            pltpu.VMEM(item_shape, BF16),
            pltpu.VMEM((samples, tokens, model), BF16),
            pltpu.VMEM((width, model), BF16),
            pltpu.VMEM((GROUP, 8, samples * local), jnp.int32),
            pltpu.VMEM(table_shape, F32),
            pltpu.VMEM(table_shape, F32),
            pltpu.VMEM(turned_shape, BF16),
            pltpu.VMEM(turned_shape, BF16),
            pltpu.VMEM((8, tokens), F32),
            pltpu.VMEM((width, model), F32),
            pltpu.VMEM((2, width, 512), BF16),
            dma((4,)),
            dma((4,)),
            dma((2, 1 + SIDE, 2, 2)),
            dma((2, 1 + SIDE, 2, 2)),
            dma((6,)),
            dma((10,)),
        ],
        compiler_params=pltpu.CompilerParams(
            collective_id=0, has_side_effects=True, vmem_limit_bytes=63 * MIB
        ),
        cost_estimate=pl.CostEstimate(
            flops=24_000_000_000, bytes_accessed=40_000_000, transcendentals=6_000_000
        ),
        name="gather_forward",
    )(query_pre, key_pre, saved_values, out_grad, out_weight, seen, table)
    weight_grad = lax.psum_scatter(partial, "dp", scatter_dimension=0, tiled=True).astype(F32)
    grads = pl.pallas_call(
        backward_kernel,
        out_shape=[jax.ShapeDtypeStruct(query_pre.shape, BF16)] * 3,
        in_specs=[hbm] * 8,
        out_specs=[hbm] * 3,
        scratch_shapes=[
            pltpu.VMEM(item_shape, BF16),
            pltpu.VMEM(item_shape, BF16),
            pltpu.VMEM(item_shape, BF16),
            pltpu.VMEM(turned_shape, BF16),
            pltpu.VMEM(turned_shape, BF16),
            pltpu.VMEM((8, tokens), F32),
            pltpu.VMEM(table_shape, F32),
            pltpu.VMEM(table_shape, F32),
            pltpu.VMEM(item_shape, BF16),
            pltpu.VMEM(item_shape, BF16),
            pltpu.VMEM(item_shape, BF16),
            pltpu.VMEM((tokens, HEAD), F32),
            pltpu.VMEM((tokens, HEAD), F32),
            pltpu.VMEM((HEAD, tokens), BF16),
            dma((samples + 1, 7)),
            dma((3,)),
            dma((3,)),
            dma((3,)),
        ],
        compiler_params=pltpu.CompilerParams(
            collective_id=1, has_side_effects=True, vmem_limit_bytes=60 * MIB
        ),
        cost_estimate=pl.CostEstimate(
            flops=40_000_000_000, bytes_accessed=20_000_000, transcendentals=6_000_000
        ),
        name="backward",
    )(q, k, v, do_t, att_t, lse, cosine, sine)
    return (*grads, weight_grad)


def solution(mesh):
    rows = P("dp", "seq", None)
    return jax.shard_map(
        body,
        mesh=mesh,
        in_specs=(rows, rows, rows, rows, P("seq", None), P("dp", "seq")),
        out_specs=(rows, rows, rows, P(("seq", "dp"), None)),
        check_vma=False,
    )
```

```python
import functools
import math

import jax
import jax.numpy as jnp
from jax import lax
from jax.experimental import pallas as pl
from jax.experimental.pallas import tpu as pltpu
from jax.sharding import PartitionSpec as P

HEAD = 128
GRID = 64
SIDE = 4
GROUP = SIDE * SIDE
MESH = pl.DeviceIdType.MESH
F32 = jnp.float32
BF16 = jnp.bfloat16
MIB = 1024 * 1024
NT = (((1,), (1,)), ((), ()))
TN = (((0,), (0,)), ((), ()))


def dot(a, b, dims=(((1,), (0,)), ((), ()))):
    return lax.dot_general(a, b, dims, preferred_element_type=F32)


def turn(x, cosine, sine):
    lane = lax.broadcasted_iota(jnp.int32, x.shape, 1)
    quarter = HEAD // 8
    ahead = pltpu.roll(x, HEAD - quarter, 1)
    behind = pltpu.roll(x, quarter, 1)
    partner = jnp.where((lane // quarter) % 2 == 0, ahead, behind)
    return x * cosine + partner * sine


def remote(src, dst, send, recv, target):
    return pltpu.make_async_remote_copy(
        src_ref=src,
        dst_ref=dst,
        send_sem=send,
        recv_sem=recv,
        device_id=target if isinstance(target, dict) else {"seq": target},
        device_id_type=MESH,
    )


def enter(me, rank=None, ranks=1):
    barrier = pltpu.get_barrier_semaphore()

    def greet(off, carry):
        pl.semaphore_signal(
            barrier, inc=1, device_id={"seq": lax.rem(me + off, GROUP)}, device_id_type=MESH
        )
        return carry

    def greet_rank(off, carry):
        pl.semaphore_signal(
            barrier, inc=1, device_id={"dp": lax.rem(rank + off, ranks)}, device_id_type=MESH
        )
        return carry

    lax.fori_loop(1, GROUP, greet, 0)
    if ranks > 1:
        lax.fori_loop(1, ranks, greet_rank, 0)
    pl.semaphore_wait(barrier, GROUP - 1 + ranks - 1)


def rows_of(block, size):
    return pl.ds(pl.multiple_of(block * size, size), size)


def gather_kernel(
    q_in, k_in, v_in, g_in, w_in, vis_in, pos_in,
    q_out, k_out, v_out, do_out, att_out, lse_out, cos_out, sin_out, wg_out,
    qb, kb, vb, gb, wb, visb, cosb, sinb, att, dot_t, lse, acc, stage,
    a2a_send, a2a_recv, ag_send, ag_recv, local_sem, out_sem, put_sem,
):
    me = lax.axis_index("seq")
    px, py = lax.rem(me, SIDE), lax.div(me, SIDE)
    samples, local = q_in.shape[0], q_in.shape[1]
    width = q_in.shape[2] // GROUP
    heads = width // HEAD
    tokens = local * GROUP
    part = tokens // SIDE
    model = g_in.shape[2]
    scale = math.log2(math.e) / math.sqrt(HEAD)

    def at(axis, delta, axis2=None, delta2=0):
        x, y = px, py
        for a, d in ((axis, delta), (axis2, delta2)):
            if a == 0:
                x = lax.rem(x + d, SIDE)
            elif a == 1:
                y = lax.rem(y + d, SIDE)
        return y * SIDE + x

    local_copies = [
        pltpu.make_async_copy(w_in, wb, local_sem.at[0]),
        pltpu.make_async_copy(g_in, gb.at[:, rows_of(me, local), :], local_sem.at[1]),
        pltpu.make_async_copy(vis_in, visb.at[me], local_sem.at[2]),
    ]
    for t, (src, dst) in enumerate(((q_in, qb), (k_in, kb), (v_in, vb))):
        local_copies.append(
            pltpu.make_async_copy(
                src.at[:, :, rows_of(me, width)], dst.at[:, rows_of(me, local), :], local_sem.at[3 + t]
            )
        )
    for copy in local_copies:
        copy.start()

    enter(me)

    dirs = (1, SIDE - 1)
    mid = local // 2

    def half_rows(block, which):
        return pl.ds(pl.multiple_of(block * local + which * mid, mid), mid)

    def ag_copy(half, slot, direction, stage_index, block, axis, from_input=False):
        if stage_index == 0:
            place = rows_of(block, local)
        else:
            place = half_rows(block, direction)
        dst = gb.at[half, place, :]
        src = g_in.at[half] if from_input else dst
        return remote(
            src, dst,
            ag_send.at[half, slot, direction, stage_index],
            ag_recv.at[half, slot, direction, stage_index],
            at(axis, dirs[direction]),
        )

    started = []

    def begin(*args, **kwargs):
        copy = ag_copy(*args, **kwargs)
        copy.start()
        started.append(copy)

    def first_direct(half, direction):
        begin(half, 0, direction, 0, me, half, from_input=True)

    def second_direct(half, b):
        for direction in range(2):
            begin(half, 1 + b, direction, 0, at(half, b), 1 - half, from_input=b == 0)

    def got_first(half, direction):
        block = at(half, SIDE - dirs[direction])
        ag_copy(half, 0, direction, 0, block, half).wait_recv()
        begin(half, 0, direction, 1, block, half)
        second_direct(half, (SIDE - dirs[direction]) % SIDE)

    def got_first_far(half):
        block = at(half, 2)
        for direction in range(2):
            ag_copy(half, 0, direction, 1, block, half).wait_recv()
        second_direct(half, 2)

    def got_second(half, b):
        for direction in range(2):
            block = at(half, b, 1 - half, SIDE - dirs[direction])
            ag_copy(half, 1 + b, direction, 0, block, 1 - half).wait_recv()
            begin(half, 1 + b, direction, 1, block, 1 - half)

    def got_second_far(half, b):
        block = at(half, b, 1 - half, 2)
        for direction in range(2):
            ag_copy(half, 1 + b, direction, 1, block, 1 - half).wait_recv()

    for half in range(2):
        for direction in range(2):
            first_direct(half, direction)
    for half in range(2):
        second_direct(half, 0)

    pairs = ((q_in, qb), (k_in, kb), (v_in, vb))

    def send_vis(off, carry):
        target = lax.rem(me + off, GROUP)
        remote(vis_in, visb.at[me], a2a_send.at[3], a2a_recv.at[3], target).start()
        return carry

    lax.fori_loop(1, GROUP, send_vis, 0)
    for t, (src, dst) in enumerate(pairs):

        def send_one(off, carry, src=src, dst=dst, t=t):
            target = lax.rem(me + off, GROUP)
            remote(
                src.at[:, :, rows_of(target, width)],
                dst.at[:, rows_of(me, local), :],
                a2a_send.at[t], a2a_recv.at[t], target,
            ).start()
            return carry

        lax.fori_loop(1, GROUP, send_one, 0)

    def a2a_wait(t, sem, ref):
        view = ref.at[:, pl.ds(0, tokens - local), :] if t < 3 else ref.at[pl.ds(0, GROUP - 1)]
        pltpu.make_async_copy(view, view, sem.at[t]).wait()

    for copy in local_copies:
        copy.wait()

    for half in range(2):
        for direction in range(2):
            got_first(half, direction)
    for half in range(2):
        got_second(half, 0)

    a2a_wait(3, a2a_recv, visb)

    def tables(src, carry):
        seen = visb[src, 0:1, :]
        row, col = lax.div(seen, GRID), lax.rem(seen, GRID)
        place = lax.broadcasted_iota(jnp.int32, (HEAD, 2 * local), 0)
        hot = jnp.where((place == row) | (place == col + GRID), 1.0, 0.0)
        both = lax.dot_general(
            hot, pos_in[...], TN, preferred_element_type=F32, precision=lax.Precision.HIGHEST
        )
        for s in range(samples):
            rows = both[s * local:(s + 1) * local]
            cosb[s, rows_of(src, local), :] = rows[:, :HEAD]
            sinb[s, rows_of(src, local), :] = rows[:, HEAD:]
        return carry

    lax.fori_loop(0, GROUP, tables, 0)
    for t, (_, dst) in enumerate(pairs):
        a2a_wait(t, a2a_recv, dst)

    chunk = 256

    def forward(s, h):
        lanes = slice(h * HEAD, (h + 1) * HEAD)
        cosine, sine = cosb[s], sinb[s]
        qb[s, :, lanes] = turn(qb[s, :, lanes].astype(F32), cosine, sine).astype(BF16)
        kb[s, :, lanes] = turn(kb[s, :, lanes].astype(F32), cosine, sine).astype(BF16)
        values_t = vb[s, :, lanes].astype(F32).T.astype(BF16)

        def one(c, carry):
            place = rows_of(c, chunk)
            scores = dot(kb[s, :, lanes], qb[s, place, lanes], NT) * scale
            top = jnp.max(scores, axis=0, keepdims=True)
            expon = jnp.exp2(scores - top)
            total = jnp.sum(expon, axis=0, keepdims=True)
            probs = (expon * (1.0 / total)).astype(BF16)
            att[s, lanes, place] = dot(values_t, probs).astype(BF16)
            lse[s * heads + h:s * heads + h + 1, place] = top + jnp.log2(total)
            return carry

        lax.fori_loop(0, tokens // chunk, one, 0)

    def out_dir(s, row):
        place = rows_of(row, part)
        dot_t[s, :, place] = dot(wb[...], gb[s, place, :], NT).astype(BF16)

    tile = stage.shape[4]

    def weight_part(row, first=False, last=False):
        place = rows_of(row, part)

        def puts(j, slot):
            return [
                pltpu.make_async_copy(
                    stage.at[slot, :, core], wg_out.at[core, :, :, rows_of(j, tile)],
                    put_sem.at[slot, core],
                )
                for core in range(2)
            ]

        def one(j, carry):
            cols = rows_of(j, tile)
            total = dot(att[0, :, place], gb[0, place, cols])
            for s in range(1, samples):
                total += dot(att[s, :, place], gb[s, place, cols])
            if not first:
                total += acc[:, cols]
            if last:
                slot = lax.rem(j, 2)

                @pl.when(j >= 2)
                def _():
                    for copy in puts(j - 2, slot):
                        copy.wait()

                stage[slot] = total.astype(BF16).reshape(stage.shape[1:])
                for copy in puts(j, slot):
                    copy.start()
            else:
                acc[:, cols] = total
            return carry

        steps = model // tile
        lax.fori_loop(0, steps, one, 0)
        if last:
            for j in (steps - 2, steps - 1):
                for copy in puts(j, j % 2):
                    copy.wait()

    near = [lax.rem(py + d, SIDE) for d in range(SIDE)]

    forward(0, 0)
    for half in range(2):
        got_first_far(half)
    forward(0, 1)
    for b in (1, SIDE - 1):
        for half in range(2):
            got_second(half, b)
        forward(*((0, 2) if b == 1 else (1, 0)))
    for half in range(2):
        got_second_far(half, 0)
    out_dir(0, near[0])
    out_dir(1, near[0])
    for half in range(2):
        got_second(half, 2)
    forward(1, 1)
    forward(1, 2)
    weight_part(near[0], first=True)
    for b in (1, SIDE - 1):
        for half in range(2):
            got_second_far(half, b)
        out_dir(0, near[b])
        out_dir(1, near[b])
        weight_part(near[b])
    outs = [
        pltpu.make_async_copy(src, dst, out_sem.at[2 + i])
        for i, (src, dst) in enumerate(
            (
                (qb, q_out), (kb, k_out), (vb, v_out), (att, att_out),
                (lse, lse_out), (cosb, cos_out), (sinb, sin_out),
            )
        )
    ]
    for copy in outs:
        copy.start()
    for half in range(2):
        got_second_far(half, 2)
    out_dir(0, near[2])
    out_dir(1, near[2])
    last = pltpu.make_async_copy(dot_t, do_out, out_sem.at[2 + len(outs)])
    last.start()
    weight_part(near[2], last=True)
    last.wait()
    for copy in outs:
        copy.wait()
    for copy in started:
        copy.wait_send()
    for t, (_, dst) in enumerate(pairs):
        a2a_wait(t, a2a_send, dst)
    a2a_wait(3, a2a_send, visb)


def backward_kernel(
    ranks,
    q_in, k_in, v_in, do_in, att_in, lse_in, cos_in, sin_in, wg_in,
    dq_out, dk_out, dv_out, wg_out,
    qb, kb, vb, dob, attb, lseb, cosb, sinb, dqb, dkb, dvb, dka, dva, kt,
    wga, wgs, wgz, wgf,
    load_sem, send_sem, recv_sem, own_sem, wg_send, wg_recv, wg_sem,
):
    me, rank = lax.axis_index("seq"), lax.axis_index("dp")
    levels = ranks // 2
    level, core = lax.div(rank, 2), lax.rem(rank, 2)
    samples, tokens, width = q_in.shape
    heads = width // HEAD
    local = tokens // GROUP
    scale = 1.0 / math.sqrt(HEAD)
    scale2 = math.log2(math.e) / math.sqrt(HEAD)
    chunk = 256

    def loads(s):
        return [
            pltpu.make_async_copy(src.at[s], dst.at[s], load_sem.at[s, i])
            for i, (src, dst) in enumerate(
                (
                    (q_in, qb), (k_in, kb), (v_in, vb), (do_in, dob),
                    (att_in, attb), (cos_in, cosb), (sin_in, sinb),
                )
            )
        ]

    shared = pltpu.make_async_copy(lse_in, lseb, load_sem.at[samples, 0])
    shared.start()
    for s in range(samples):
        for copy in loads(s):
            copy.start()
    own_part = pltpu.make_async_copy(wg_in.at[core], wga, wg_sem.at[0])
    own_part.start()
    enter(me, rank, ranks)

    to_core = remote(
        wg_in.at[1 - core], wgs, wg_send.at[0], wg_recv.at[0], {"dp": level * 2 + 1 - core}
    )
    to_core.start()

    def to_level(off):
        target = lax.rem(level + off, levels)
        return remote(
            wga.at[target], wgz.at[off - 1], wg_send.at[off], wg_recv.at[off],
            {"dp": target * 2 + core},
        )

    done = pltpu.make_async_copy(wgf, wg_out, wg_sem.at[1])
    model = wga.shape[2]
    piece = 512

    def add_cores():
        own_part.wait()
        to_core.wait_recv()

        def one(c, carry):
            cols = rows_of(c, piece)
            wga[:, :, cols] = (
                wga[:, :, cols].astype(F32) + wgs[:, :, cols].astype(F32)
            ).astype(BF16)
            return carry

        lax.fori_loop(0, model // piece, one, 0)
        for off in range(1, levels):
            to_level(off).start()

    def add_levels():
        for off in range(1, levels):
            to_level(off).wait_recv()

        def one(c, carry):
            cols = rows_of(c, piece)
            total = wga[level, :, cols].astype(F32)
            for off in range(1, levels):
                total += wgz[off - 1, :, cols].astype(F32)
            wgf[:, cols] = total
            return carry

        lax.fori_loop(0, model // piece, one, 0)
        done.start()

    shared.wait()

    outs = ((dqb, dq_out), (dkb, dk_out), (dvb, dv_out))

    def item(s, h):
        lanes = slice(h * HEAD, (h + 1) * HEAD)
        row = s * heads + h
        kt[...] = kb[s, :, lanes].astype(F32).T.astype(BF16)
        dka[...] = jnp.zeros_like(dka)
        dva[...] = jnp.zeros_like(dva)

        def one(c, carry):
            place = rows_of(c, chunk)
            queries = qb[s, place, lanes]
            scores = dot(kb[s, :, lanes], queries, NT)
            probs = jnp.exp2(scores * scale2 - lseb[row:row + 1, place])
            into_t = dob[s, lanes, place]
            into_f = into_t.astype(F32)
            into = into_f.T.astype(BF16)
            row_dot = jnp.sum(into_f * attb[s, lanes, place].astype(F32), axis=0, keepdims=True)
            dprobs = dot(vb[s, :, lanes], into_t)
            dscores = (probs * (dprobs - row_dot)).astype(BF16)
            dva[...] += dot(probs.astype(BF16), into)
            dka[...] += dot(dscores, queries)
            dq = (dot(kt[...], dscores).T * scale).astype(BF16).astype(F32)
            dqb[s, place, lanes] = turn(dq, cosb[s, place, :], -sinb[s, place, :]).astype(BF16)
            return carry

        lax.fori_loop(0, tokens // chunk, one, 0)
        dvb[s, :, lanes] = dva[...].astype(BF16)
        dk = (dka[...] * scale).astype(BF16).astype(F32)
        dkb[s, :, lanes] = turn(dk, cosb[s], -sinb[s]).astype(BF16)

    def ship(s, h, count):
        lanes = slice(h * HEAD, (h + count) * HEAD)
        cols = pl.ds(pl.multiple_of(me * width + h * HEAD, HEAD), count * HEAD)
        for t, (src, dst) in enumerate(outs):

            def send_one(off, carry, src=src, dst=dst, t=t):
                target = lax.rem(me + off, GROUP)
                remote(
                    src.at[s, rows_of(target, local), lanes], dst.at[s, :, cols],
                    send_sem.at[t], recv_sem.at[t], target,
                ).start()
                return carry

            lax.fori_loop(1, GROUP, send_one, 0)
            pltpu.make_async_copy(
                src.at[s, rows_of(me, local), lanes], dst.at[s, :, cols], own_sem.at[t]
            ).start()

    for s in range(samples):
        for copy in loads(s):
            copy.wait()
        for h in range(heads):
            item(s, h)
            ship(s, h, 1)
            if (s, h) == (0, 0):
                add_cores()
    add_levels()

    for t, (src, dst) in enumerate(outs):
        own = dst.at[:, :, pl.ds(0, width)]
        pltpu.make_async_copy(own, own, own_sem.at[t]).wait()
        rest = dst.at[:, :, pl.ds(width, (GROUP - 1) * width)]
        pltpu.make_async_copy(rest, rest, recv_sem.at[t]).wait()
        pltpu.make_async_copy(rest, rest, send_sem.at[t]).wait()
    to_core.wait_send()
    for off in range(1, levels):
        to_level(off).wait_send()
    done.wait()


def position_table():
    quarter = HEAD // 8
    frequency = jnp.exp(jnp.arange(quarter, dtype=F32) * (-math.log(100.0) / quarter))
    angle = jnp.arange(GRID, dtype=F32)[:, None] * frequency
    cosine, sine = jnp.cos(angle), jnp.sin(angle)
    none = jnp.zeros((GRID, 2 * quarter), F32)
    rest = jnp.zeros((GRID, HEAD - 4 * quarter), F32)
    row_cos = jnp.concatenate([cosine, cosine, none, rest + 1.0], axis=1)
    col_cos = jnp.concatenate([none, cosine, cosine, rest], axis=1)
    row_sin = jnp.concatenate([-sine, sine, none, rest], axis=1)
    col_sin = jnp.concatenate([none, -sine, sine, rest], axis=1)
    return jnp.concatenate(
        [
            jnp.concatenate([row_cos, row_sin], axis=1),
            jnp.concatenate([col_cos, col_sin], axis=1),
        ],
        axis=0,
    )


def body(query_pre, key_pre, saved_values, out_grad, out_weight, visible):
    samples, local, model = query_pre.shape
    width = model // GROUP
    tokens = local * GROUP
    hbm = pl.BlockSpec(memory_space=pl.ANY)
    vmem = pl.BlockSpec(memory_space=pltpu.VMEM)
    seen = jnp.broadcast_to(visible.reshape(1, samples * local), (8, samples * local))
    item_shape = (samples, tokens, width)
    turned_shape = (samples, width, tokens)
    table_shape = (samples, tokens, HEAD)
    ranks = lax.axis_size("dp")
    partial_shape = (2, ranks // 2, width // ranks, model)
    table = position_table()
    dma = pltpu.SemaphoreType.DMA
    q, k, v, do_t, att_t, lse, cosine, sine, partial = pl.pallas_call(
        gather_kernel,
        out_shape=[
            jax.ShapeDtypeStruct(item_shape, BF16),
            jax.ShapeDtypeStruct(item_shape, BF16),
            jax.ShapeDtypeStruct(item_shape, BF16),
            jax.ShapeDtypeStruct(turned_shape, BF16),
            jax.ShapeDtypeStruct(turned_shape, BF16),
            jax.ShapeDtypeStruct((8, tokens), F32),
            jax.ShapeDtypeStruct(table_shape, F32),
            jax.ShapeDtypeStruct(table_shape, F32),
            jax.ShapeDtypeStruct(partial_shape, BF16),
        ],
        in_specs=[hbm] * 6 + [vmem],
        out_specs=[hbm] * 9,
        scratch_shapes=[
            pltpu.VMEM(item_shape, BF16),
            pltpu.VMEM(item_shape, BF16),
            pltpu.VMEM(item_shape, BF16),
            pltpu.VMEM((samples, tokens, model), BF16),
            pltpu.VMEM((width, model), BF16),
            pltpu.VMEM((GROUP, 8, samples * local), jnp.int32),
            pltpu.VMEM(table_shape, F32),
            pltpu.VMEM(table_shape, F32),
            pltpu.VMEM(turned_shape, BF16),
            pltpu.VMEM(turned_shape, BF16),
            pltpu.VMEM((8, tokens), F32),
            pltpu.VMEM((width, model), F32),
            pltpu.VMEM((2, ranks // 2, 2, width // ranks, 512), BF16),
            dma((4,)),
            dma((4,)),
            dma((2, 1 + SIDE, 2, 2)),
            dma((2, 1 + SIDE, 2, 2)),
            dma((6,)),
            dma((10,)),
            dma((2, 2)),
        ],
        compiler_params=pltpu.CompilerParams(
            collective_id=0, has_side_effects=True, vmem_limit_bytes=63 * MIB
        ),
        cost_estimate=pl.CostEstimate(
            flops=24_000_000_000, bytes_accessed=40_000_000, transcendentals=6_000_000
        ),
        name="gather_forward",
    )(query_pre, key_pre, saved_values, out_grad, out_weight, seen, table)
    return pl.pallas_call(
        functools.partial(backward_kernel, ranks),
        out_shape=[jax.ShapeDtypeStruct(query_pre.shape, BF16)] * 3
        + [jax.ShapeDtypeStruct(partial_shape[2:], F32)],
        in_specs=[hbm] * 9,
        out_specs=[hbm] * 4,
        scratch_shapes=[
            pltpu.VMEM(item_shape, BF16),
            pltpu.VMEM(item_shape, BF16),
            pltpu.VMEM(item_shape, BF16),
            pltpu.VMEM(turned_shape, BF16),
            pltpu.VMEM(turned_shape, BF16),
            pltpu.VMEM((8, tokens), F32),
            pltpu.VMEM(table_shape, F32),
            pltpu.VMEM(table_shape, F32),
            pltpu.VMEM(item_shape, BF16),
            pltpu.VMEM(item_shape, BF16),
            pltpu.VMEM(item_shape, BF16),
            pltpu.VMEM((tokens, HEAD), F32),
            pltpu.VMEM((tokens, HEAD), F32),
            pltpu.VMEM((HEAD, tokens), BF16),
            pltpu.VMEM(partial_shape[1:], BF16),
            pltpu.VMEM(partial_shape[1:], BF16),
            pltpu.VMEM((ranks // 2 - 1, *partial_shape[2:]), BF16),
            pltpu.VMEM(partial_shape[2:], F32),
            dma((samples + 1, 7)),
            dma((3,)),
            dma((3,)),
            dma((3,)),
            dma((ranks // 2,)),
            dma((ranks // 2,)),
            dma((2,)),
        ],
        compiler_params=pltpu.CompilerParams(
            collective_id=1, has_side_effects=True, vmem_limit_bytes=60 * MIB
        ),
        cost_estimate=pl.CostEstimate(
            flops=40_000_000_000, bytes_accessed=20_000_000, transcendentals=6_000_000
        ),
        name="backward",
    )(q, k, v, do_t, att_t, lse, cosine, sine, partial)


def solution(mesh):
    rows = P("dp", "seq", None)
    return jax.shard_map(
        body,
        mesh=mesh,
        in_specs=(rows, rows, rows, rows, P("seq", None), P("dp", "seq")),
        out_specs=(rows, rows, rows, P(("seq", "dp"), None)),
        check_vma=False,
    )
```

```python
import functools
import math

import jax
import jax.numpy as jnp
from jax import lax
from jax.experimental import pallas as pl
from jax.experimental.pallas import tpu as pltpu
from jax.sharding import PartitionSpec as P

HEAD = 128
GRID = 64
SIDE = 4
GROUP = SIDE * SIDE
MESH = pl.DeviceIdType.MESH
F32 = jnp.float32
BF16 = jnp.bfloat16
MIB = 1024 * 1024
NT = (((1,), (1,)), ((), ()))
TN = (((0,), (0,)), ((), ()))


def dot(a, b, dims=(((1,), (0,)), ((), ()))):
    return lax.dot_general(a, b, dims, preferred_element_type=F32)


def turn(x, cosine, sine):
    lane = lax.broadcasted_iota(jnp.int32, x.shape, 1)
    quarter = HEAD // 8
    ahead = pltpu.roll(x, HEAD - quarter, 1)
    behind = pltpu.roll(x, quarter, 1)
    partner = jnp.where((lane // quarter) % 2 == 0, ahead, behind)
    return x * cosine + partner * sine


def remote(src, dst, send, recv, target):
    return pltpu.make_async_remote_copy(
        src_ref=src,
        dst_ref=dst,
        send_sem=send,
        recv_sem=recv,
        device_id=target if isinstance(target, dict) else {"seq": target},
        device_id_type=MESH,
    )


def enter(me, rank=None, ranks=1):
    barrier = pltpu.get_barrier_semaphore()

    def greet(off, carry):
        pl.semaphore_signal(
            barrier, inc=1, device_id={"seq": lax.rem(me + off, GROUP)}, device_id_type=MESH
        )
        return carry

    def greet_rank(off, carry):
        pl.semaphore_signal(
            barrier, inc=1, device_id={"dp": lax.rem(rank + off, ranks)}, device_id_type=MESH
        )
        return carry

    lax.fori_loop(1, GROUP, greet, 0)
    if ranks > 1:
        lax.fori_loop(1, ranks, greet_rank, 0)
    pl.semaphore_wait(barrier, GROUP - 1 + ranks - 1)


def rows_of(block, size):
    return pl.ds(pl.multiple_of(block * size, size), size)


def gather_kernel(
    q_in, k_in, v_in, g_in, w_in, vis_in, pos_in,
    q_out, k_out, v_out, do_out, att_out, lse_out, cos_out, sin_out, wg_out,
    qb, kb, vb, gb, wb, visb, cosb, sinb, att, dot_t, lse, acc, stage,
    a2a_send, a2a_recv, ag_send, ag_recv, local_sem, out_sem, put_sem,
):
    me = lax.axis_index("seq")
    px, py = lax.rem(me, SIDE), lax.div(me, SIDE)
    samples, local = q_in.shape[0], q_in.shape[1]
    width = q_in.shape[2] // GROUP
    heads = width // HEAD
    tokens = local * GROUP
    part = tokens // SIDE
    model = g_in.shape[2]
    scale = math.log2(math.e) / math.sqrt(HEAD)

    def at(axis, delta, axis2=None, delta2=0):
        x, y = px, py
        for a, d in ((axis, delta), (axis2, delta2)):
            if a == 0:
                x = lax.rem(x + d, SIDE)
            elif a == 1:
                y = lax.rem(y + d, SIDE)
        return y * SIDE + x

    local_copies = [
        pltpu.make_async_copy(w_in, wb, local_sem.at[0]),
        pltpu.make_async_copy(g_in, gb.at[:, rows_of(me, local), :], local_sem.at[1]),
        pltpu.make_async_copy(vis_in, visb.at[me], local_sem.at[2]),
    ]
    for t, (src, dst) in enumerate(((q_in, qb), (k_in, kb), (v_in, vb))):
        local_copies.append(
            pltpu.make_async_copy(
                src.at[:, :, rows_of(me, width)], dst.at[:, rows_of(me, local), :], local_sem.at[3 + t]
            )
        )
    for copy in local_copies:
        copy.start()

    enter(me)

    dirs = (1, SIDE - 1)
    mid = local // 2

    def half_rows(block, which):
        return pl.ds(pl.multiple_of(block * local + which * mid, mid), mid)

    def ag_copy(half, slot, direction, stage_index, block, axis, from_input=False):
        if stage_index == 0:
            place = rows_of(block, local)
        else:
            place = half_rows(block, direction)
        dst = gb.at[half, place, :]
        src = g_in.at[half] if from_input else dst
        return remote(
            src, dst,
            ag_send.at[half, slot, direction, stage_index],
            ag_recv.at[half, slot, direction, stage_index],
            at(axis, dirs[direction]),
        )

    started = []

    def begin(*args, **kwargs):
        copy = ag_copy(*args, **kwargs)
        copy.start()
        started.append(copy)

    def first_direct(half, direction):
        begin(half, 0, direction, 0, me, half, from_input=True)

    def second_direct(half, b):
        for direction in range(2):
            begin(half, 1 + b, direction, 0, at(half, b), 1 - half, from_input=b == 0)

    def got_first(half, direction):
        block = at(half, SIDE - dirs[direction])
        ag_copy(half, 0, direction, 0, block, half).wait_recv()
        begin(half, 0, direction, 1, block, half)
        second_direct(half, (SIDE - dirs[direction]) % SIDE)

    def got_first_far(half):
        block = at(half, 2)
        for direction in range(2):
            ag_copy(half, 0, direction, 1, block, half).wait_recv()
        second_direct(half, 2)

    def got_second(half, b):
        for direction in range(2):
            block = at(half, b, 1 - half, SIDE - dirs[direction])
            ag_copy(half, 1 + b, direction, 0, block, 1 - half).wait_recv()
            begin(half, 1 + b, direction, 1, block, 1 - half)

    def got_second_far(half, b):
        block = at(half, b, 1 - half, 2)
        for direction in range(2):
            ag_copy(half, 1 + b, direction, 1, block, 1 - half).wait_recv()

    for half in range(2):
        for direction in range(2):
            first_direct(half, direction)
    for half in range(2):
        second_direct(half, 0)

    pairs = ((q_in, qb), (k_in, kb), (v_in, vb))

    def send_vis(off, carry):
        target = lax.rem(me + off, GROUP)
        remote(vis_in, visb.at[me], a2a_send.at[3], a2a_recv.at[3], target).start()
        return carry

    lax.fori_loop(1, GROUP, send_vis, 0)
    for t, (src, dst) in enumerate(pairs):

        def send_one(off, carry, src=src, dst=dst, t=t):
            target = lax.rem(me + off, GROUP)
            remote(
                src.at[:, :, rows_of(target, width)],
                dst.at[:, rows_of(me, local), :],
                a2a_send.at[t], a2a_recv.at[t], target,
            ).start()
            return carry

        lax.fori_loop(1, GROUP, send_one, 0)

    def a2a_wait(t, sem, ref):
        view = ref.at[:, pl.ds(0, tokens - local), :] if t < 3 else ref.at[pl.ds(0, GROUP - 1)]
        pltpu.make_async_copy(view, view, sem.at[t]).wait()

    for copy in local_copies:
        copy.wait()

    for half in range(2):
        for direction in range(2):
            got_first(half, direction)
    for half in range(2):
        got_second(half, 0)

    a2a_wait(3, a2a_recv, visb)

    def tables(src, carry):
        seen = visb[src, 0:1, :]
        row, col = lax.div(seen, GRID), lax.rem(seen, GRID)
        place = lax.broadcasted_iota(jnp.int32, (HEAD, 2 * local), 0)
        hot = jnp.where((place == row) | (place == col + GRID), 1.0, 0.0)
        both = lax.dot_general(
            hot, pos_in[...], TN, preferred_element_type=F32, precision=lax.Precision.HIGHEST
        )
        for s in range(samples):
            rows = both[s * local:(s + 1) * local]
            cosb[s, rows_of(src, local), :] = rows[:, :HEAD]
            sinb[s, rows_of(src, local), :] = rows[:, HEAD:]
        return carry

    lax.fori_loop(0, GROUP, tables, 0)
    for t, (_, dst) in enumerate(pairs):
        a2a_wait(t, a2a_recv, dst)

    chunk = 256

    def forward(s, h):
        lanes = slice(h * HEAD, (h + 1) * HEAD)
        cosine, sine = cosb[s], sinb[s]
        qb[s, :, lanes] = turn(qb[s, :, lanes].astype(F32), cosine, sine).astype(BF16)
        kb[s, :, lanes] = turn(kb[s, :, lanes].astype(F32), cosine, sine).astype(BF16)
        values_t = vb[s, :, lanes].astype(F32).T.astype(BF16)

        def one(c, carry):
            place = rows_of(c, chunk)
            scores = dot(kb[s, :, lanes], qb[s, place, lanes], NT) * scale
            top = jnp.max(scores, axis=0, keepdims=True)
            expon = jnp.exp2(scores - top)
            total = jnp.sum(expon, axis=0, keepdims=True)
            probs = (expon * (1.0 / total)).astype(BF16)
            att[s, lanes, place] = dot(values_t, probs).astype(BF16)
            lse[s * heads + h:s * heads + h + 1, place] = top + jnp.log2(total)
            return carry

        lax.fori_loop(0, tokens // chunk, one, 0)

    def out_dir(s, row):
        place = rows_of(row, part)
        dot_t[s, :, place] = dot(wb[...], gb[s, place, :], NT).astype(BF16)

    tile = stage.shape[4]

    def weight_part(row, first=False, last=False):
        place = rows_of(row, part)

        def puts(j, slot):
            return [
                pltpu.make_async_copy(
                    stage.at[slot, :, core], wg_out.at[core, :, :, rows_of(j, tile)],
                    put_sem.at[slot, core],
                )
                for core in range(2)
            ]

        def one(j, carry):
            cols = rows_of(j, tile)
            total = dot(att[0, :, place], gb[0, place, cols])
            for s in range(1, samples):
                total += dot(att[s, :, place], gb[s, place, cols])
            if not first:
                total += acc[:, cols]
            if last:
                slot = lax.rem(j, 2)

                @pl.when(j >= 2)
                def _():
                    for copy in puts(j - 2, slot):
                        copy.wait()

                stage[slot] = total.astype(BF16).reshape(stage.shape[1:])
                for copy in puts(j, slot):
                    copy.start()
            else:
                acc[:, cols] = total
            return carry

        steps = model // tile
        lax.fori_loop(0, steps, one, 0)
        if last:
            for j in (steps - 2, steps - 1):
                for copy in puts(j, j % 2):
                    copy.wait()

    near = [lax.rem(py + d, SIDE) for d in range(SIDE)]

    forward(0, 0)
    for half in range(2):
        got_first_far(half)
    forward(0, 1)
    for b in (1, SIDE - 1):
        for half in range(2):
            got_second(half, b)
        forward(*((0, 2) if b == 1 else (1, 0)))
    for half in range(2):
        got_second_far(half, 0)
    out_dir(0, near[0])
    out_dir(1, near[0])
    for half in range(2):
        got_second(half, 2)
    forward(1, 1)
    forward(1, 2)
    weight_part(near[0], first=True)
    for b in (1, SIDE - 1):
        for half in range(2):
            got_second_far(half, b)
        out_dir(0, near[b])
        out_dir(1, near[b])
        weight_part(near[b])
    outs = [
        pltpu.make_async_copy(src, dst, out_sem.at[2 + i])
        for i, (src, dst) in enumerate(
            (
                (qb, q_out), (kb, k_out), (vb, v_out), (att, att_out),
                (lse, lse_out), (cosb, cos_out), (sinb, sin_out),
            )
        )
    ]
    for copy in outs:
        copy.start()
    for half in range(2):
        got_second_far(half, 2)
    out_dir(0, near[2])
    out_dir(1, near[2])
    last = pltpu.make_async_copy(dot_t, do_out, out_sem.at[2 + len(outs)])
    last.start()
    weight_part(near[2], last=True)
    last.wait()
    for copy in outs:
        copy.wait()
    for copy in started:
        copy.wait_send()
    for t, (_, dst) in enumerate(pairs):
        a2a_wait(t, a2a_send, dst)
    a2a_wait(3, a2a_send, visb)


def backward_kernel(
    ranks,
    q_in, k_in, v_in, do_in, att_in, lse_in, cos_in, sin_in, wg_in,
    dq_out, dk_out, dv_out, wg_out,
    qb, kb, vb, dob, attb, lseb, cosb, sinb, dqb, dkb, dvb, dka, dva, kt,
    wga, wgs, wgz, wgf,
    load_sem, send_sem, recv_sem, own_sem, wg_send, wg_recv, wg_sem,
):
    me, rank = lax.axis_index("seq"), lax.axis_index("dp")
    levels = ranks // 2
    level, core = lax.div(rank, 2), lax.rem(rank, 2)
    samples, tokens, width = q_in.shape
    heads = width // HEAD
    local = tokens // GROUP
    scale = 1.0 / math.sqrt(HEAD)
    scale2 = math.log2(math.e) / math.sqrt(HEAD)
    chunk = 256

    def loads(s):
        return [
            pltpu.make_async_copy(src.at[s], dst.at[s], load_sem.at[s, i])
            for i, (src, dst) in enumerate(
                (
                    (q_in, qb), (k_in, kb), (v_in, vb), (do_in, dob),
                    (att_in, attb), (cos_in, cosb), (sin_in, sinb),
                )
            )
        ]

    shared = pltpu.make_async_copy(lse_in, lseb, load_sem.at[samples, 0])
    shared.start()
    for s in range(samples):
        for copy in loads(s):
            copy.start()
    own_part = pltpu.make_async_copy(wg_in.at[core], wga, wg_sem.at[0])
    own_part.start()
    enter(me, rank, ranks)

    to_core = remote(
        wg_in.at[1 - core], wgs, wg_send.at[0], wg_recv.at[0], {"dp": level * 2 + 1 - core}
    )
    to_core.start()

    def to_level(off):
        target = lax.rem(level + off, levels)
        return remote(
            wga.at[target], wgz.at[off - 1], wg_send.at[off], wg_recv.at[off],
            {"dp": target * 2 + core},
        )

    done = pltpu.make_async_copy(wgf, wg_out, wg_sem.at[1])
    model = wga.shape[2]
    piece = 512

    def add_cores():
        own_part.wait()
        to_core.wait_recv()

        def one(c, carry):
            cols = rows_of(c, piece)
            wga[:, :, cols] = (
                wga[:, :, cols].astype(F32) + wgs[:, :, cols].astype(F32)
            ).astype(BF16)
            return carry

        lax.fori_loop(0, model // piece, one, 0)
        for off in range(1, levels):
            to_level(off).start()

    def add_levels():
        for off in range(1, levels):
            to_level(off).wait_recv()

        def one(c, carry):
            cols = rows_of(c, piece)
            total = wga[level, :, cols].astype(F32)
            for off in range(1, levels):
                total += wgz[off - 1, :, cols].astype(F32)
            wgf[:, cols] = total
            return carry

        lax.fori_loop(0, model // piece, one, 0)
        done.start()

    shared.wait()

    outs = ((dqb, dq_out), (dkb, dk_out), (dvb, dv_out))

    def item(s, h):
        lanes = slice(h * HEAD, (h + 1) * HEAD)
        row = s * heads + h
        kt[...] = kb[s, :, lanes].astype(F32).T.astype(BF16)
        dka[...] = jnp.zeros_like(dka)
        dva[...] = jnp.zeros_like(dva)

        def one(c, carry):
            place = rows_of(c, chunk)
            queries = qb[s, place, lanes]
            scores = dot(kb[s, :, lanes], queries, NT)
            probs = jnp.exp2(scores * scale2 - lseb[row:row + 1, place])
            into_t = dob[s, lanes, place]
            into_f = into_t.astype(F32)
            into = into_f.T.astype(BF16)
            row_dot = jnp.sum(into_f * attb[s, lanes, place].astype(F32), axis=0, keepdims=True)
            dprobs = dot(vb[s, :, lanes], into_t)
            dscores = (probs * (dprobs - row_dot)).astype(BF16)
            dva[...] += dot(probs.astype(BF16), into)
            dka[...] += dot(dscores, queries)
            dq = (dot(kt[...], dscores).T * scale).astype(BF16).astype(F32)
            dqb[s, place, lanes] = turn(dq, cosb[s, place, :], -sinb[s, place, :]).astype(BF16)
            return carry

        lax.fori_loop(0, tokens // chunk, one, 0)
        dvb[s, :, lanes] = dva[...].astype(BF16)
        dk = (dka[...] * scale).astype(BF16).astype(F32)
        dkb[s, :, lanes] = turn(dk, cosb[s], -sinb[s]).astype(BF16)

    def ship(s, h, count):
        lanes = slice(h * HEAD, (h + count) * HEAD)
        cols = pl.ds(pl.multiple_of(me * width + h * HEAD, HEAD), count * HEAD)
        for t, (src, dst) in enumerate(outs):

            def send_one(off, carry, src=src, dst=dst, t=t):
                target = lax.rem(me + off, GROUP)
                remote(
                    src.at[s, rows_of(target, local), lanes], dst.at[s, :, cols],
                    send_sem.at[t], recv_sem.at[t], target,
                ).start()
                return carry

            lax.fori_loop(1, GROUP, send_one, 0)
            pltpu.make_async_copy(
                src.at[s, rows_of(me, local), lanes], dst.at[s, :, cols], own_sem.at[t]
            ).start()

    for s in range(samples):
        for copy in loads(s):
            copy.wait()
        for h in range(heads):
            item(s, h)
            ship(s, h, 1)
            if (s, h) == (0, 0):
                add_cores()
    add_levels()

    for t, (src, dst) in enumerate(outs):
        own = dst.at[:, :, pl.ds(0, width)]
        pltpu.make_async_copy(own, own, own_sem.at[t]).wait()
        rest = dst.at[:, :, pl.ds(width, (GROUP - 1) * width)]
        pltpu.make_async_copy(rest, rest, recv_sem.at[t]).wait()
        pltpu.make_async_copy(rest, rest, send_sem.at[t]).wait()
    to_core.wait_send()
    for off in range(1, levels):
        to_level(off).wait_send()
    done.wait()


def position_table():
    quarter = HEAD // 8
    frequency = jnp.exp(jnp.arange(quarter, dtype=F32) * (-math.log(100.0) / quarter))
    angle = jnp.arange(GRID, dtype=F32)[:, None] * frequency
    cosine, sine = jnp.cos(angle), jnp.sin(angle)
    none = jnp.zeros((GRID, 2 * quarter), F32)
    rest = jnp.zeros((GRID, HEAD - 4 * quarter), F32)
    row_cos = jnp.concatenate([cosine, cosine, none, rest + 1.0], axis=1)
    col_cos = jnp.concatenate([none, cosine, cosine, rest], axis=1)
    row_sin = jnp.concatenate([-sine, sine, none, rest], axis=1)
    col_sin = jnp.concatenate([none, -sine, sine, rest], axis=1)
    return jnp.concatenate(
        [
            jnp.concatenate([row_cos, row_sin], axis=1),
            jnp.concatenate([col_cos, col_sin], axis=1),
        ],
        axis=0,
    )


def body(query_pre, key_pre, saved_values, out_grad, out_weight, visible):
    samples, local, model = query_pre.shape
    width = model // GROUP
    tokens = local * GROUP
    hbm = pl.BlockSpec(memory_space=pl.ANY)
    vmem = pl.BlockSpec(memory_space=pltpu.VMEM)
    seen = jnp.broadcast_to(visible.reshape(1, samples * local), (8, samples * local))
    item_shape = (samples, tokens, width)
    turned_shape = (samples, width, tokens)
    table_shape = (samples, tokens, HEAD)
    ranks = lax.axis_size("dp")
    partial_shape = (2, ranks // 2, width // ranks, model)
    table = position_table()
    dma = pltpu.SemaphoreType.DMA
    q, k, v, do_t, att_t, lse, cosine, sine, partial = pl.pallas_call(
        gather_kernel,
        out_shape=[
            jax.ShapeDtypeStruct(item_shape, BF16),
            jax.ShapeDtypeStruct(item_shape, BF16),
            jax.ShapeDtypeStruct(item_shape, BF16),
            jax.ShapeDtypeStruct(turned_shape, BF16),
            jax.ShapeDtypeStruct(turned_shape, BF16),
            jax.ShapeDtypeStruct((8, tokens), F32),
            jax.ShapeDtypeStruct(table_shape, F32),
            jax.ShapeDtypeStruct(table_shape, F32),
            jax.ShapeDtypeStruct(partial_shape, BF16),
        ],
        in_specs=[hbm] * 6 + [vmem],
        out_specs=[hbm] * 9,
        scratch_shapes=[
            pltpu.VMEM(item_shape, BF16),
            pltpu.VMEM(item_shape, BF16),
            pltpu.VMEM(item_shape, BF16),
            pltpu.VMEM((samples, tokens, model), BF16),
            pltpu.VMEM((width, model), BF16),
            pltpu.VMEM((GROUP, 8, samples * local), jnp.int32),
            pltpu.VMEM(table_shape, F32),
            pltpu.VMEM(table_shape, F32),
            pltpu.VMEM(turned_shape, BF16),
            pltpu.VMEM(turned_shape, BF16),
            pltpu.VMEM((8, tokens), F32),
            pltpu.VMEM((width, model), F32),
            pltpu.VMEM((2, ranks // 2, 2, width // ranks, 1024), BF16),
            dma((4,)),
            dma((4,)),
            dma((2, 1 + SIDE, 2, 2)),
            dma((2, 1 + SIDE, 2, 2)),
            dma((6,)),
            dma((10,)),
            dma((2, 2)),
        ],
        compiler_params=pltpu.CompilerParams(
            collective_id=0, has_side_effects=True, vmem_limit_bytes=63 * MIB
        ),
        cost_estimate=pl.CostEstimate(
            flops=24_000_000_000, bytes_accessed=40_000_000, transcendentals=6_000_000
        ),
        name="gather_forward",
    )(query_pre, key_pre, saved_values, out_grad, out_weight, seen, table)
    return pl.pallas_call(
        functools.partial(backward_kernel, ranks),
        out_shape=[jax.ShapeDtypeStruct(query_pre.shape, BF16)] * 3
        + [jax.ShapeDtypeStruct(partial_shape[2:], F32)],
        in_specs=[hbm] * 9,
        out_specs=[hbm] * 4,
        scratch_shapes=[
            pltpu.VMEM(item_shape, BF16),
            pltpu.VMEM(item_shape, BF16),
            pltpu.VMEM(item_shape, BF16),
            pltpu.VMEM(turned_shape, BF16),
            pltpu.VMEM(turned_shape, BF16),
            pltpu.VMEM((8, tokens), F32),
            pltpu.VMEM(table_shape, F32),
            pltpu.VMEM(table_shape, F32),
            pltpu.VMEM(item_shape, BF16),
            pltpu.VMEM(item_shape, BF16),
            pltpu.VMEM(item_shape, BF16),
            pltpu.VMEM((tokens, HEAD), F32),
            pltpu.VMEM((tokens, HEAD), F32),
            pltpu.VMEM((HEAD, tokens), BF16),
            pltpu.VMEM(partial_shape[1:], BF16),
            pltpu.VMEM(partial_shape[1:], BF16),
            pltpu.VMEM((ranks // 2 - 1, *partial_shape[2:]), BF16),
            pltpu.VMEM(partial_shape[2:], F32),
            dma((samples + 1, 7)),
            dma((3,)),
            dma((3,)),
            dma((3,)),
            dma((ranks // 2,)),
            dma((ranks // 2,)),
            dma((2,)),
        ],
        compiler_params=pltpu.CompilerParams(
            collective_id=1, has_side_effects=True, vmem_limit_bytes=60 * MIB
        ),
        cost_estimate=pl.CostEstimate(
            flops=40_000_000_000, bytes_accessed=20_000_000, transcendentals=6_000_000
        ),
        name="backward",
    )(q, k, v, do_t, att_t, lse, cosine, sine, partial)


def solution(mesh):
    rows = P("dp", "seq", None)
    return jax.shard_map(
        body,
        mesh=mesh,
        in_specs=(rows, rows, rows, rows, P("seq", None), P("dp", "seq")),
        out_specs=(rows, rows, rows, P(("seq", "dp"), None)),
        check_vma=False,
    )
```

```python
import functools
import math

import jax
import jax.numpy as jnp
import numpy as np
from jax import lax
from jax.experimental import pallas as pl
from jax.experimental.pallas import tpu as pltpu
from jax.sharding import PartitionSpec as P

HEAD = 128
GRID = 64
SIDE = 4
GROUP = SIDE * SIDE
MESH = pl.DeviceIdType.MESH
F32 = jnp.float32
BF16 = jnp.bfloat16
MIB = 1024 * 1024
NT = (((1,), (1,)), ((), ()))
TN = (((0,), (0,)), ((), ()))


def dot(a, b, dims=(((1,), (0,)), ((), ()))):
    return lax.dot_general(a, b, dims, preferred_element_type=F32)


def turn(x, cosine, sine):
    lane = lax.broadcasted_iota(jnp.int32, x.shape, 1)
    quarter = HEAD // 8
    ahead = pltpu.roll(x, HEAD - quarter, 1)
    behind = pltpu.roll(x, quarter, 1)
    partner = jnp.where((lane // quarter) % 2 == 0, ahead, behind)
    return x * cosine + partner * sine


def remote(src, dst, send, recv, target):
    return pltpu.make_async_remote_copy(
        src_ref=src,
        dst_ref=dst,
        send_sem=send,
        recv_sem=recv,
        device_id=target if isinstance(target, dict) else {"seq": target},
        device_id_type=MESH,
    )


def enter(me, rank=None, ranks=1):
    barrier = pltpu.get_barrier_semaphore()

    def greet(off, carry):
        pl.semaphore_signal(
            barrier, inc=1, device_id={"seq": lax.rem(me + off, GROUP)}, device_id_type=MESH
        )
        return carry

    def greet_rank(off, carry):
        pl.semaphore_signal(
            barrier, inc=1, device_id={"dp": lax.rem(rank + off, ranks)}, device_id_type=MESH
        )
        return carry

    lax.fori_loop(1, GROUP, greet, 0)
    if ranks > 1:
        lax.fori_loop(1, ranks, greet_rank, 0)
    pl.semaphore_wait(barrier, GROUP - 1 + ranks - 1)


def rows_of(block, size):
    return pl.ds(pl.multiple_of(block * size, size), size)


def gather_kernel(
    q_in, k_in, v_in, g_in, w_in, vis_in, pos_in,
    q_out, k_out, v_out, do_out, att_out, lse_out, cos_out, sin_out, wg_out,
    qb, kb, vb, gb, wb, visb, cosb, sinb, att, dot_t, lse, acc, stage,
    a2a_send, a2a_recv, ag_send, ag_recv, local_sem, out_sem, put_sem,
):
    me = lax.axis_index("seq")
    px, py = lax.rem(me, SIDE), lax.div(me, SIDE)
    samples, local = q_in.shape[0], q_in.shape[1]
    width = q_in.shape[2] // GROUP
    heads = width // HEAD
    tokens = local * GROUP
    part = tokens // SIDE
    model = g_in.shape[2]
    scale = math.log2(math.e) / math.sqrt(HEAD)

    def at(axis, delta, axis2=None, delta2=0):
        x, y = px, py
        for a, d in ((axis, delta), (axis2, delta2)):
            if a == 0:
                x = lax.rem(x + d, SIDE)
            elif a == 1:
                y = lax.rem(y + d, SIDE)
        return y * SIDE + x

    local_copies = [
        pltpu.make_async_copy(w_in, wb, local_sem.at[0]),
        pltpu.make_async_copy(g_in, gb.at[:, rows_of(me, local), :], local_sem.at[1]),
        pltpu.make_async_copy(vis_in, visb.at[me], local_sem.at[2]),
    ]
    for t, (src, dst) in enumerate(((q_in, qb), (k_in, kb), (v_in, vb))):
        local_copies.append(
            pltpu.make_async_copy(
                src.at[:, :, rows_of(me, width)], dst.at[:, rows_of(me, local), :], local_sem.at[3 + t]
            )
        )
    for copy in local_copies:
        copy.start()

    enter(me)

    dirs = (1, SIDE - 1)
    mid = local // 2

    def half_rows(block, which):
        return pl.ds(pl.multiple_of(block * local + which * mid, mid), mid)

    def ag_copy(half, slot, direction, stage_index, block, axis, from_input=False):
        if stage_index == 0:
            place = rows_of(block, local)
        else:
            place = half_rows(block, direction)
        dst = gb.at[half, place, :]
        src = g_in.at[half] if from_input else dst
        return remote(
            src, dst,
            ag_send.at[half, slot, direction, stage_index],
            ag_recv.at[half, slot, direction, stage_index],
            at(axis, dirs[direction]),
        )

    started = []

    def begin(*args, **kwargs):
        copy = ag_copy(*args, **kwargs)
        copy.start()
        started.append(copy)

    def first_direct(half, direction):
        begin(half, 0, direction, 0, me, half, from_input=True)

    def second_direct(half, b):
        for direction in range(2):
            begin(half, 1 + b, direction, 0, at(half, b), 1 - half, from_input=b == 0)

    def got_first(half, direction):
        block = at(half, SIDE - dirs[direction])
        ag_copy(half, 0, direction, 0, block, half).wait_recv()
        begin(half, 0, direction, 1, block, half)
        second_direct(half, (SIDE - dirs[direction]) % SIDE)

    def got_first_far(half):
        block = at(half, 2)
        for direction in range(2):
            ag_copy(half, 0, direction, 1, block, half).wait_recv()
        second_direct(half, 2)

    def got_second(half, b):
        for direction in range(2):
            block = at(half, b, 1 - half, SIDE - dirs[direction])
            ag_copy(half, 1 + b, direction, 0, block, 1 - half).wait_recv()
            begin(half, 1 + b, direction, 1, block, 1 - half)

    def got_second_far(half, b):
        block = at(half, b, 1 - half, 2)
        for direction in range(2):
            ag_copy(half, 1 + b, direction, 1, block, 1 - half).wait_recv()

    for half in range(2):
        for direction in range(2):
            first_direct(half, direction)
    for half in range(2):
        second_direct(half, 0)

    pairs = ((q_in, qb), (k_in, kb), (v_in, vb))

    def send_vis(off, carry):
        target = lax.rem(me + off, GROUP)
        remote(vis_in, visb.at[me], a2a_send.at[3], a2a_recv.at[3], target).start()
        return carry

    lax.fori_loop(1, GROUP, send_vis, 0)
    for t, (src, dst) in enumerate(pairs):

        def send_one(off, carry, src=src, dst=dst, t=t):
            target = lax.rem(me + off, GROUP)
            remote(
                src.at[:, :, rows_of(target, width)],
                dst.at[:, rows_of(me, local), :],
                a2a_send.at[t], a2a_recv.at[t], target,
            ).start()
            return carry

        lax.fori_loop(1, GROUP, send_one, 0)

    def a2a_wait(t, sem, ref):
        view = ref.at[:, pl.ds(0, tokens - local), :] if t < 3 else ref.at[pl.ds(0, GROUP - 1)]
        pltpu.make_async_copy(view, view, sem.at[t]).wait()

    for copy in local_copies:
        copy.wait()

    for half in range(2):
        for direction in range(2):
            got_first(half, direction)
    for half in range(2):
        got_second(half, 0)

    a2a_wait(3, a2a_recv, visb)

    def tables(src, carry):
        seen = visb[src, 0:1, :]
        row, col = lax.div(seen, GRID), lax.rem(seen, GRID)
        place = lax.broadcasted_iota(jnp.int32, (HEAD, 2 * local), 0)
        hot = jnp.where((place == row) | (place == col + GRID), 1.0, 0.0)
        both = lax.dot_general(
            hot, pos_in[...], TN, preferred_element_type=F32, precision=lax.Precision.HIGHEST
        )
        for s in range(samples):
            rows = both[s * local:(s + 1) * local]
            cosb[s, rows_of(src, local), :] = rows[:, :HEAD]
            sinb[s, rows_of(src, local), :] = rows[:, HEAD:]
        return carry

    lax.fori_loop(0, GROUP, tables, 0)
    for t, (_, dst) in enumerate(pairs):
        a2a_wait(t, a2a_recv, dst)

    chunk = 256

    def forward(s, h):
        lanes = slice(h * HEAD, (h + 1) * HEAD)
        cosine, sine = cosb[s], sinb[s]
        qb[s, :, lanes] = turn(qb[s, :, lanes].astype(F32), cosine, sine).astype(BF16)
        kb[s, :, lanes] = turn(kb[s, :, lanes].astype(F32), cosine, sine).astype(BF16)
        values_t = vb[s, :, lanes].astype(F32).T.astype(BF16)

        def one(c, carry):
            place = rows_of(c, chunk)
            scores = dot(kb[s, :, lanes], qb[s, place, lanes], NT) * scale
            top = jnp.max(scores, axis=0, keepdims=True)
            expon = jnp.exp2(scores - top)
            total = jnp.sum(expon, axis=0, keepdims=True)
            probs = (expon * (1.0 / total)).astype(BF16)
            att[s, lanes, place] = dot(values_t, probs).astype(BF16)
            lse[s * heads + h:s * heads + h + 1, place] = top + jnp.log2(total)
            return carry

        lax.fori_loop(0, tokens // chunk, one, 0)

    def out_dir(s, row):
        place = rows_of(row, part)
        dot_t[s, :, place] = dot(wb[...], gb[s, place, :], NT).astype(BF16)

    tile = stage.shape[4]

    def weight_part(row, first=False, last=False):
        place = rows_of(row, part)

        def puts(j, slot):
            return [
                pltpu.make_async_copy(
                    stage.at[slot, :, core], wg_out.at[core, :, :, rows_of(j, tile)],
                    put_sem.at[slot, core],
                )
                for core in range(2)
            ]

        def one(j, carry):
            cols = rows_of(j, tile)
            total = dot(att[0, :, place], gb[0, place, cols])
            for s in range(1, samples):
                total += dot(att[s, :, place], gb[s, place, cols])
            if not first:
                total += acc[:, cols]
            if last:
                slot = lax.rem(j, 2)

                @pl.when(j >= 2)
                def _():
                    for copy in puts(j - 2, slot):
                        copy.wait()

                stage[slot] = total.astype(BF16).reshape(stage.shape[1:])
                for copy in puts(j, slot):
                    copy.start()
            else:
                acc[:, cols] = total
            return carry

        steps = model // tile
        lax.fori_loop(0, steps, one, 0)
        if last:
            for j in (steps - 2, steps - 1):
                for copy in puts(j, j % 2):
                    copy.wait()

    near = [lax.rem(py + d, SIDE) for d in range(SIDE)]

    forward(0, 0)
    for half in range(2):
        got_first_far(half)
    forward(0, 1)
    for b in (1, SIDE - 1):
        for half in range(2):
            got_second(half, b)
        forward(*((0, 2) if b == 1 else (1, 0)))
    for half in range(2):
        got_second_far(half, 0)
    out_dir(0, near[0])
    out_dir(1, near[0])
    for half in range(2):
        got_second(half, 2)
    forward(1, 1)
    forward(1, 2)
    weight_part(near[0], first=True)
    for b in (1, SIDE - 1):
        for half in range(2):
            got_second_far(half, b)
        out_dir(0, near[b])
        out_dir(1, near[b])
        weight_part(near[b])
    outs = [
        pltpu.make_async_copy(src, dst, out_sem.at[2 + i])
        for i, (src, dst) in enumerate(
            (
                (qb, q_out), (kb, k_out), (vb, v_out), (att, att_out),
                (lse, lse_out), (cosb, cos_out), (sinb, sin_out),
            )
        )
    ]
    for copy in outs:
        copy.start()
    for half in range(2):
        got_second_far(half, 2)
    out_dir(0, near[2])
    out_dir(1, near[2])
    last = pltpu.make_async_copy(dot_t, do_out, out_sem.at[2 + len(outs)])
    last.start()
    weight_part(near[2], last=True)
    last.wait()
    for copy in outs:
        copy.wait()
    for copy in started:
        copy.wait_send()
    for t, (_, dst) in enumerate(pairs):
        a2a_wait(t, a2a_send, dst)
    a2a_wait(3, a2a_send, visb)


def backward_kernel(
    ranks,
    q_in, k_in, v_in, do_in, att_in, lse_in, cos_in, sin_in, wg_in,
    dq_out, dk_out, dv_out, wg_out,
    qb, kb, vb, dob, attb, lseb, cosb, sinb, dqb, dkb, dvb, dka, dva, kt,
    wga, wgs,
    load_sem, send_sem, recv_sem, own_sem, wg_send, wg_recv, wg_sem,
):
    me, rank = lax.axis_index("seq"), lax.axis_index("dp")
    levels = ranks // 2
    level, core = lax.div(rank, 2), lax.rem(rank, 2)
    samples, tokens, width = q_in.shape
    heads = width // HEAD
    local = tokens // GROUP
    scale = 1.0 / math.sqrt(HEAD)
    scale2 = math.log2(math.e) / math.sqrt(HEAD)
    chunk = 256

    def loads(s):
        return [
            pltpu.make_async_copy(src.at[s], dst.at[s], load_sem.at[s, i])
            for i, (src, dst) in enumerate(
                (
                    (q_in, qb), (k_in, kb), (v_in, vb), (do_in, dob),
                    (att_in, attb), (cos_in, cosb), (sin_in, sinb),
                )
            )
        ]

    shared = pltpu.make_async_copy(lse_in, lseb, load_sem.at[samples, 0])
    shared.start()
    for s in range(samples):
        for copy in loads(s):
            copy.start()
    own_part = pltpu.make_async_copy(wg_in.at[core], wga, wg_sem.at[0])
    own_part.start()
    enter(me, rank, ranks)

    to_core = remote(
        wg_in.at[1 - core], wgs, wg_send.at[0], wg_recv.at[0], {"dp": level * 2 + 1 - core}
    )
    to_core.start()

    def to_level(off):
        target = lax.rem(level + off, levels)
        return remote(
            wga.at[target], wg_out.at[off], wg_send.at[off], wg_recv.at[off],
            {"dp": target * 2 + core},
        )

    own_share = pltpu.make_async_copy(wga.at[level], wg_out.at[0], wg_sem.at[1])
    model = wga.shape[2]
    piece = 512

    def add_cores():
        own_part.wait()
        to_core.wait_recv()

        def one(c, carry):
            cols = rows_of(c, piece)
            wga[:, :, cols] = (
                wga[:, :, cols].astype(F32) + wgs[:, :, cols].astype(F32)
            ).astype(BF16)
            return carry

        lax.fori_loop(0, model // piece, one, 0)
        own_share.start()
        for off in range(1, levels):
            to_level(off).start()

    shared.wait()

    outs = ((dqb, dq_out), (dkb, dk_out), (dvb, dv_out))

    def item(s, h):
        lanes = slice(h * HEAD, (h + 1) * HEAD)
        row = s * heads + h
        kt[...] = kb[s, :, lanes].astype(F32).T.astype(BF16)
        dka[...] = jnp.zeros_like(dka)
        dva[...] = jnp.zeros_like(dva)

        def one(c, carry):
            place = rows_of(c, chunk)
            queries = qb[s, place, lanes]
            scores = dot(kb[s, :, lanes], queries, NT)
            probs = jnp.exp2(scores * scale2 - lseb[row:row + 1, place])
            into_t = dob[s, lanes, place]
            into_f = into_t.astype(F32)
            into = into_f.T.astype(BF16)
            row_dot = jnp.sum(into_f * attb[s, lanes, place].astype(F32), axis=0, keepdims=True)
            dprobs = dot(vb[s, :, lanes], into_t)
            dscores = (probs * (dprobs - row_dot)).astype(BF16)
            dva[...] += dot(probs.astype(BF16), into)
            dka[...] += dot(dscores, queries)
            dq = (dot(kt[...], dscores).T * scale).astype(BF16).astype(F32)
            dqb[s, place, lanes] = turn(dq, cosb[s, place, :], -sinb[s, place, :]).astype(BF16)
            return carry

        lax.fori_loop(0, tokens // chunk, one, 0)
        dvb[s, :, lanes] = dva[...].astype(BF16)
        dk = (dka[...] * scale).astype(BF16).astype(F32)
        dkb[s, :, lanes] = turn(dk, cosb[s], -sinb[s]).astype(BF16)

    def ship(s, h, count):
        lanes = slice(h * HEAD, (h + count) * HEAD)
        cols = pl.ds(pl.multiple_of(me * width + h * HEAD, HEAD), count * HEAD)
        for t, (src, dst) in enumerate(outs):

            def send_one(off, carry, src=src, dst=dst, t=t):
                target = lax.rem(me + off, GROUP)
                remote(
                    src.at[s, rows_of(target, local), lanes], dst.at[s, :, cols],
                    send_sem.at[t], recv_sem.at[t], target,
                ).start()
                return carry

            lax.fori_loop(1, GROUP, send_one, 0)
            pltpu.make_async_copy(
                src.at[s, rows_of(me, local), lanes], dst.at[s, :, cols], own_sem.at[t]
            ).start()

    for s in range(samples):
        for copy in loads(s):
            copy.wait()
        for h in range(heads):
            item(s, h)
            ship(s, h, 1)
            if (s, h) == (0, 0):
                add_cores()

    for t, (src, dst) in enumerate(outs):
        own = dst.at[:, :, pl.ds(0, width)]
        pltpu.make_async_copy(own, own, own_sem.at[t]).wait()
        rest = dst.at[:, :, pl.ds(width, (GROUP - 1) * width)]
        pltpu.make_async_copy(rest, rest, recv_sem.at[t]).wait()
        pltpu.make_async_copy(rest, rest, send_sem.at[t]).wait()
    to_core.wait_send()
    for off in range(1, levels):
        to_level(off).wait()
    own_share.wait()


def position_table():
    quarter = HEAD // 8
    frequency = 100.0 ** (-np.arange(quarter) / quarter)
    angle = np.arange(GRID)[:, None] * frequency
    cosine, sine = np.cos(angle), np.sin(angle)
    none = np.zeros((GRID, 2 * quarter))
    rest = np.zeros((GRID, HEAD - 4 * quarter))
    row = np.concatenate([cosine, cosine, none, rest + 1.0, -sine, sine, none, rest], axis=1)
    col = np.concatenate([none, cosine, cosine, rest, none, -sine, sine, rest], axis=1)
    return jnp.asarray(np.concatenate([row, col], axis=0), F32)


def body(query_pre, key_pre, saved_values, out_grad, out_weight, visible):
    samples, local, model = query_pre.shape
    width = model // GROUP
    tokens = local * GROUP
    hbm = pl.BlockSpec(memory_space=pl.ANY)
    vmem = pl.BlockSpec(memory_space=pltpu.VMEM)
    seen = jnp.broadcast_to(visible.reshape(1, samples * local), (8, samples * local))
    item_shape = (samples, tokens, width)
    turned_shape = (samples, width, tokens)
    table_shape = (samples, tokens, HEAD)
    ranks = lax.axis_size("dp")
    partial_shape = (2, ranks // 2, width // ranks, model)
    table = position_table()
    dma = pltpu.SemaphoreType.DMA
    q, k, v, do_t, att_t, lse, cosine, sine, partial = pl.pallas_call(
        gather_kernel,
        out_shape=[
            jax.ShapeDtypeStruct(item_shape, BF16),
            jax.ShapeDtypeStruct(item_shape, BF16),
            jax.ShapeDtypeStruct(item_shape, BF16),
            jax.ShapeDtypeStruct(turned_shape, BF16),
            jax.ShapeDtypeStruct(turned_shape, BF16),
            jax.ShapeDtypeStruct((8, tokens), F32),
            jax.ShapeDtypeStruct(table_shape, F32),
            jax.ShapeDtypeStruct(table_shape, F32),
            jax.ShapeDtypeStruct(partial_shape, BF16),
        ],
        in_specs=[hbm] * 6 + [vmem],
        out_specs=[hbm] * 9,
        scratch_shapes=[
            pltpu.VMEM(item_shape, BF16),
            pltpu.VMEM(item_shape, BF16),
            pltpu.VMEM(item_shape, BF16),
            pltpu.VMEM((samples, tokens, model), BF16),
            pltpu.VMEM((width, model), BF16),
            pltpu.VMEM((GROUP, 8, samples * local), jnp.int32),
            pltpu.VMEM(table_shape, F32),
            pltpu.VMEM(table_shape, F32),
            pltpu.VMEM(turned_shape, BF16),
            pltpu.VMEM(turned_shape, BF16),
            pltpu.VMEM((8, tokens), F32),
            pltpu.VMEM((width, model), F32),
            pltpu.VMEM((2, ranks // 2, 2, width // ranks, 1024), BF16),
            dma((4,)),
            dma((4,)),
            dma((2, 1 + SIDE, 2, 2)),
            dma((2, 1 + SIDE, 2, 2)),
            dma((6,)),
            dma((10,)),
            dma((2, 2)),
        ],
        compiler_params=pltpu.CompilerParams(
            collective_id=0, has_side_effects=True, vmem_limit_bytes=63 * MIB
        ),
        cost_estimate=pl.CostEstimate(
            flops=24_000_000_000, bytes_accessed=40_000_000, transcendentals=6_000_000
        ),
        name="gather_forward",
    )(query_pre, key_pre, saved_values, out_grad, out_weight, seen, table)
    *grads, shares = pl.pallas_call(
        functools.partial(backward_kernel, ranks),
        out_shape=[jax.ShapeDtypeStruct(query_pre.shape, BF16)] * 3
        + [jax.ShapeDtypeStruct(partial_shape[1:], BF16)],
        in_specs=[hbm] * 9,
        out_specs=[hbm] * 4,
        scratch_shapes=[
            pltpu.VMEM(item_shape, BF16),
            pltpu.VMEM(item_shape, BF16),
            pltpu.VMEM(item_shape, BF16),
            pltpu.VMEM(turned_shape, BF16),
            pltpu.VMEM(turned_shape, BF16),
            pltpu.VMEM((8, tokens), F32),
            pltpu.VMEM(table_shape, F32),
            pltpu.VMEM(table_shape, F32),
            pltpu.VMEM(item_shape, BF16),
            pltpu.VMEM(item_shape, BF16),
            pltpu.VMEM(item_shape, BF16),
            pltpu.VMEM((tokens, HEAD), F32),
            pltpu.VMEM((tokens, HEAD), F32),
            pltpu.VMEM((HEAD, tokens), BF16),
            pltpu.VMEM(partial_shape[1:], BF16),
            pltpu.VMEM(partial_shape[1:], BF16),
            dma((samples + 1, 7)),
            dma((3,)),
            dma((3,)),
            dma((3,)),
            dma((ranks // 2,)),
            dma((ranks // 2,)),
            dma((2,)),
        ],
        compiler_params=pltpu.CompilerParams(
            collective_id=1, has_side_effects=True, vmem_limit_bytes=60 * MIB
        ),
        cost_estimate=pl.CostEstimate(
            flops=40_000_000_000, bytes_accessed=20_000_000, transcendentals=6_000_000
        ),
        name="backward",
    )(q, k, v, do_t, att_t, lse, cosine, sine, partial)
    return (*grads, jnp.sum(shares.astype(F32), axis=0))


def solution(mesh):
    rows = P("dp", "seq", None)
    return jax.shard_map(
        body,
        mesh=mesh,
        in_specs=(rows, rows, rows, rows, P("seq", None), P("dp", "seq")),
        out_specs=(rows, rows, rows, P(("seq", "dp"), None)),
        check_vma=False,
    )
```
